128 devices in a mesh: ens: 8 (over y, core), space: 16 (over z, x).
Axes of the slice: x: 4, y: 4, z: 4, core: 2. Of those that a mesh axis runs over, the one named last changes fastest.
Arguments:
- prior_profiles: bfloat16 [256, 128, 64, 128], P('ens', 'space'), may hold values from -6 to 6
- conductivity_profile: bfloat16 [256, 128, 64, 128], P('ens', 'space'), may hold values from 0.5 to 2
- sensor_position_flat: int32 [16384], P('space'), may hold values from 0 to 65535
- observation_slot_count: int32 [16], P('space'), may hold values from 1 to 1024, 10240 in all
- obs_values: float32 [16384], P('space'), may hold values from -6 to 6
- obs_std: float32 [16384], P('space'), may hold values from 0.3 to 3
- obs_noise: float32 [256, 16384], P('ens', 'space'), may hold values from -6 to 6
- params: float32 [256, 2048], P('ens', 'space'), may hold values from -6 to 6
Outputs:
- posterior_parameters: float32 [256, 2048], P('ens', 'space')
- predicted_states: float32 [256, 128, 64, 128], P('ens', 'space')
The draws below stay inside these ranges and needn't reach their ends.
Inputs may be any that keep to these rules, and one draw needn't show every extreme that they name: The live slots of a slab are its first observation_slot_count ones.
All inputs are finite; a program needn't handle non-finite values. No bound on the sum of `observation_slot_count` on one device may be relied on, other than what follows from the above.
Results may differ from the reference program's by a relative error of at most 0.0003.
Values may be sent and summed in bfloat16 or wider, within the bound.
No kernel may reach another device: no remote copies, remote signals or barrier semaphores. Data moves between devices by JAX's collectives and lax.ppermute only.
A program may use at most 256 MiB of HBM per device.

```python
import math
import jax
import jax.numpy as jnp
import numpy as np
from jax import lax

M = 256
CZ = 8
NX = 64
NY = 128
NZ = 128
P_SIZE = 2048
OBS_CAP = 1024
OBS = 16384
N_SPACE = 16


def touch_ends(values, key, least, largest):
    spot = [jax.random.randint(jax.random.fold_in(key, axis), (), 0, length) for axis, length in enumerate(values.shape)]
    widest = values.shape.index(max(values.shape))
    beside = spot[:widest] + [(spot[widest] + 1) % values.shape[widest]] + spot[widest + 1:]
    return values.at[tuple(spot)].set(least).at[tuple(beside)].set(largest)


def block_scale(stream_key, shape, cuts, smallest, top_value):
    level = 1.0
    for dim, shards_of in cuts:
        heights = jax.random.uniform(jax.random.fold_in(jax.random.fold_in(stream_key, 6), dim), (shards_of,), jnp.float32, smallest / len(cuts), top_value / len(cuts))
        level = level * jnp.repeat(jnp.exp(heights), shape[dim] // shards_of).reshape((-1,) + (1,) * (len(shape) - 1 - dim))
    return level


def profile(amount, total, limit, lean):
    weights = [(1 << 20) // math.isqrt(standing ** lean) + 1 for standing in range(2, amount + 1)]
    surplus, given = total - limit - (amount - 1), [1] * (amount - 1)
    while surplus > 0:
        movable = [i for i in range(amount - 1) if given[i] < limit]
        mass, left = sum([weights[i] for i in movable]), surplus
        for i in movable:
            addition = min(limit - given[i], max(1, left * weights[i] // mass), surplus)
            given[i] = given[i] + addition
            surplus = surplus - addition
    return np.array([limit] + given)


def ragged(own_key, amount, total, most, slope):
    if amount == 2:
        one = jax.random.randint(own_key, (), max(1, total - most), min(most, total - 1) + 1)
        return jnp.stack([one, total - one])
    sizes = jnp.asarray(profile(amount, total, most, slope), jnp.int32)
    twos = (amount - 1) // 2
    source_of, receiver = sizes[1:1 + 2 * twos:2], sizes[2:2 + 2 * twos:2]
    slack = jnp.minimum(source_of - 1, most - receiver)
    passed = jax.random.randint(jax.random.fold_in(own_key, 1), (twos,), 0, 1 << 20) % (slack + 1)
    sizes = sizes.at[1:1 + 2 * twos:2].set(source_of - passed).at[2:2 + 2 * twos:2].set(receiver + passed)
    return sizes[jax.random.permutation(jax.random.fold_in(own_key, 2), amount)]


def centred(stream_key, shape, width, limit, shards=(), held_as=jnp.bfloat16):
    values = width * jax.random.normal(stream_key, shape, jnp.float32)
    if shards:
        values = values * block_scale(stream_key, shape, shards, -0.22, 0.18)
    return jnp.clip(values, -limit, limit).astype(held_as)


def setup_inputs(seed: int = 0) -> dict:
    seeds = jax.random.split(jax.random.key(seed), 9)
    return {
        "prior_profiles": centred(seeds[0], (M, NZ, NX, NY), 1.0, 6.0, ((0, 8), (1, 16))),
        "conductivity_profile": jnp.clip(jnp.exp(math.log(2.0) - 1.3862944 * jax.random.uniform(seeds[1], (M, NZ, NX, NY), jnp.float32) ** block_scale(seeds[1], (M, NZ, NX, NY), ((0, 8), (1, 16)), -0.2, 0.2)), 0.5, 2.0).astype(jnp.bfloat16),
        "sensor_position_flat": touch_ends(jax.random.randint(seeds[2], (OBS,), 0, CZ * NX * NY), jax.random.fold_in(seeds[2], 1), 0, (CZ * NX * NY) - 1).astype(jnp.int32),
        "observation_slot_count": ragged(seeds[3], N_SPACE, N_SPACE * OBS_CAP * 5 // 8, OBS_CAP, 2).astype(jnp.int32),
        "obs_values": centred(seeds[4], (OBS,), 1.0, 6.0, ((0, 16),), jnp.float32),
        "obs_std": jnp.clip(jnp.exp(math.log(3.0) - 2.3025851 * jax.random.uniform(seeds[5], (OBS,), jnp.float32) ** block_scale(seeds[5], (OBS,), ((0, 16),), -0.2, 0.2)), 0.3, 3.0),
        "obs_noise": centred(seeds[6], (M, OBS), 1.0, 6.0, ((0, 8), (1, 16)), jnp.float32),
        "params": centred(seeds[7], (M, P_SIZE), 1.0, 6.0, ((0, 8), (1, 16)), jnp.float32),
    }


step_size = 0.08

def inner_window(array, starts):
    for dimension in range(3):
        which_axis = array.ndim - 3 + dimension
        extent = array.shape[which_axis] - 2
        array = lax.slice_in_dim(array, starts[dimension], starts[dimension] + extent, axis=which_axis)
    return array

def spread_heat_onestep(field, coeff):
    centre_u = inner_window(field, (1, 1, 1))
    centre_k = inner_window(coeff, (1, 1, 1))
    flux = jnp.zeros_like(centre_u)
    for dimension in range(3):
        for offset in (0, 2):
            starts = [1, 1, 1]
            starts[dimension] = offset
            neigh_u = inner_window(field, tuple(starts))
            neigh_k = inner_window(coeff, tuple(starts))
            flux = flux + 0.5 * (centre_k + neigh_k) * (neigh_u - centre_u)
    return centre_u + step_size * flux

def reference(prior_profiles, conductivity_profile, sensor_position_flat, observation_slot_count, obs_values, obs_std, obs_noise, params):
    cell_table = sensor_position_flat.reshape(N_SPACE, OBS_CAP)

    def realization_march(pair):
        field = jnp.pad(pair[0].astype(jnp.float32), 1)
        coeff = jnp.pad(pair[1].astype(jnp.float32), 1)
        result = spread_heat_onestep(field, coeff)
        slabs = result.reshape(N_SPACE, CZ * NX * NY)
        selected_members = jnp.take_along_axis(slabs, cell_table, axis=1).reshape(OBS)
        return (result, selected_members)
    predicted_states, sampled_readings = lax.map(realization_march, (prior_profiles, conductivity_profile))
    slot_index = jnp.arange(OBS, dtype=jnp.int32) % OBS_CAP
    live_slots = slot_index < jnp.repeat(observation_slot_count, OBS_CAP)
    ens_scale = math.sqrt(M - 1.0)
    centre = lax.optimization_barrier(jnp.mean(sampled_readings, axis=0))
    spread = jnp.where(live_slots, (sampled_readings - centre) / (obs_std * ens_scale), 0.0)
    misfit = jnp.where(live_slots, (obs_values - sampled_readings) / obs_std + obs_noise, 0.0)
    gram_matrix = jnp.dot(spread, spread.T, precision=lax.Precision.HIGHEST)
    cross_term = jnp.dot(spread, misfit.T, precision=lax.Precision.HIGHEST)
    factor = jnp.linalg.cholesky(gram_matrix + jnp.eye(M, dtype=jnp.float32))
    weights = jax.scipy.linalg.cho_solve((factor, True), cross_term)
    anomaly = (params - lax.optimization_barrier(jnp.mean(params, axis=0))) / ens_scale
    posterior_parameters = params + jnp.dot(weights.T, anomaly, precision=lax.Precision.HIGHEST)
    return (posterior_parameters, predicted_states)
```

```python
import math

import jax
import jax.numpy as jnp
from jax import lax
from jax.experimental import pallas as pl
from jax.experimental.pallas import tpu as pltpu
from jax.sharding import PartitionSpec as P

step_size = 0.08
HIGH = lax.Precision.HIGHEST
F32 = jnp.float32


def shift_down(a, first):
    return jnp.concatenate([first, a[:-1]], axis=0)


def shift_up(a):
    return jnp.concatenate([a[1:], jnp.zeros_like(a[:1])], axis=0)


def sample(pos_ref, src_ref, dst_ref, stride, place, initial=None):
    members, slots = dst_ref.shape
    groups = members // 8
    lane = lax.broadcasted_iota(jnp.int32, (8, 128), 1)

    def block(jb, _):
        def chunk(jc, accs):
            accs = list(accs)
            for t in range(8):
                j = jc * 8 + t
                p = pos_ref[jb * 128 + j]
                row, used = place(p)
                target = j if used is None else jnp.where(used, j, -1)
                turn = (j - p) & 127
                here = lane == target
                for g in range(groups):
                    v = src_ref[pl.ds(g * 8 * stride + row, 8, stride=stride), :]
                    accs[g] = jnp.where(here, pltpu.roll(v, turn, 1), accs[g])
            return tuple(accs)

        at = pl.ds(pl.multiple_of(jb * 128, 128), 128)
        if initial is None:
            start = tuple(jnp.zeros((8, 128), F32) for _ in range(groups))
        else:
            start = tuple(jnp.zeros((8, 128), F32) for _ in range(groups))
        accs = lax.fori_loop(0, 16, chunk, start)
        for g in range(groups):
            value = accs[g]
            if initial is not None:
                value = value + initial[g * 8 : g * 8 + 8, at]
            dst_ref[g * 8 : g * 8 + 8, at] = value
        return 0

    lax.fori_loop(0, slots // 128, block, 0)


def stencil_kernel(pos_ref, u_ref, k_ref, out_ref, picked_ref, state, sem):
    i = pl.program_id(0)
    members, layers, nx, ny = u_ref.shape
    lane = lax.broadcasted_iota(jnp.int32, (nx, ny), 1)
    first_lane, last_lane = lane == 0, lane == ny - 1
    half = step_size * 0.5

    def member(b, _):
        base = (i * members + b) * layers * nx
        u = u_ref[b, 0].astype(F32)
        k = k_ref[b, 0].astype(F32)
        below = None
        for z in range(layers):
            ku = k * u
            un = jnp.where(last_lane, 0.0, pltpu.roll(u, ny - 1, 1))
            kn = jnp.where(last_lane, 0.0, pltpu.roll(k, ny - 1, 1))
            f = (k + kn) * (un - u)
            acc = f - jnp.where(first_lane, ku, pltpu.roll(f, 1, 1))
            f = (k + shift_up(k)) * (shift_up(u) - u)
            acc = acc + (f - shift_down(f, ku[:1]))
            if below is not None:
                acc = acc - below
            u_now = u
            if z < layers - 1:
                u_next = u_ref[b, z + 1].astype(F32)
                k_next = k_ref[b, z + 1].astype(F32)
                below = (k + k_next) * (u_next - u)
                acc = acc + below
                u, k = u_next, k_next
            state[pl.ds(pl.multiple_of(base + z * nx, 8), nx), :] = u_now + half * acc
        return 0

    lax.fori_loop(0, members, member, 0)
    rows = members * layers * nx

    def push(step):
        part = pl.ds(pl.multiple_of(step * rows, 8), rows)
        return pltpu.make_async_copy(state.at[part, :], out_ref.at[part, :], sem.at[step])

    push(i).start()

    @pl.when(i == pl.num_programs(0) - 1)
    def _():
        sample(pos_ref, state, picked_ref, layers * nx, lambda p: (p >> 7, None))
        for step in range(state.shape[0] // rows):
            push(step).wait()


def stencil(pos, u, k):
    m, layers, nx, ny = u.shape
    per = 4
    block = pl.BlockSpec((per, layers, nx, ny), lambda i: (i, 0, 0, 0))
    rows = m * layers * nx
    return pl.pallas_call(
        stencil_kernel,
        grid=(m // per,),
        in_specs=[pl.BlockSpec(memory_space=pltpu.SMEM), block, block],
        out_specs=[
            pl.BlockSpec(memory_space=pl.ANY),
            pl.BlockSpec((m, pos.shape[0]), lambda i: (0, 0)),
        ],
        out_shape=[
            jax.ShapeDtypeStruct((rows, ny), F32),
            jax.ShapeDtypeStruct((m, pos.shape[0]), F32),
        ],
        scratch_shapes=[pltpu.VMEM((rows, ny), F32), pltpu.SemaphoreType.DMA((m // per,))],
        compiler_params=pltpu.CompilerParams(vmem_limit_bytes=32 << 20),
        cost_estimate=pl.CostEstimate(
            flops=40 * u.size, bytes_accessed=8 * u.size, transcendentals=0
        ),
    )(pos, u, k)


def faces_kernel(pos_ref, u_ref, k_ref, lo_ref, hi_ref, in_ref, partial_ref, out_ref, picked_ref, extra):
    g, side = pl.program_id(0), pl.program_id(1)
    members, _, nx, ny = u_ref.shape
    half = step_size * 0.5

    def apply(halo):
        def member(b, _):
            u = u_ref[b, 0].astype(F32)
            k = k_ref[b, 0].astype(F32)
            un = halo[0, b].astype(F32)
            kn = halo[1, b].astype(F32)
            d = half * ((k + kn) * (un - u))
            out_ref[b, 0] = in_ref[b, 0] + d
            at = ((g * members + b) * 2 + side) * nx
            extra[pl.ds(pl.multiple_of(at, 8), nx), :] = d
            return 0

        lax.fori_loop(0, members, member, 0)

    @pl.when(side == 0)
    def _():
        apply(lo_ref)

    @pl.when(side == 1)
    def _():
        apply(hi_ref)

    def place(p):
        z = p >> 13
        return ((z >> 2) << 6) + ((p >> 7) & 63), (z == 0) | (z == 7)

    @pl.when((g == pl.num_programs(0) - 1) & (side == 1))
    def _():
        sample(pos_ref, extra, picked_ref, 2 * nx, place, partial_ref)


def faces(pos, u, k, lo, hi, states, partial):
    m, layers, nx, ny = u.shape
    per = 8
    face = pl.BlockSpec((per, 1, nx, ny), lambda g, s: (g, s * (layers - 1), 0, 0))
    halo = pl.BlockSpec((2, per, nx, ny), lambda g, s: (0, g, 0, 0))
    flat = pl.BlockSpec(partial.shape, lambda g, s: (0, 0))
    return pl.pallas_call(
        faces_kernel,
        grid=(m // per, 2),
        in_specs=[pl.BlockSpec(memory_space=pltpu.SMEM), face, face, halo, halo, face, flat],
        out_specs=[face, flat],
        out_shape=[
            jax.ShapeDtypeStruct(states.shape, F32),
            jax.ShapeDtypeStruct(partial.shape, F32),
        ],
        scratch_shapes=[pltpu.VMEM((m * 2 * nx, ny), F32)],
        input_output_aliases={5: 0},
        compiler_params=pltpu.CompilerParams(vmem_limit_bytes=32 << 20),
        cost_estimate=pl.CostEstimate(
            flops=8 * m * nx * ny, bytes_accessed=24 * m * nx * ny, transcendentals=0
        ),
    )(pos, u, k, lo, hi, states, partial)


def contract(a, b, dims):
    return lax.dot_general(a, b, (dims, ((), ())), precision=HIGH, preferred_element_type=F32)


def gram_kernel(scale, count_ref, *refs):
    blocks, (noise, values, std, gram_ref, cross_ref) = refs[:8], refs[8:]
    rows = blocks[0].shape[0]
    own = blocks[0][...]
    total = own
    for b in blocks[1:]:
        total = total + b[...]
    centre = jnp.sum(total, axis=0, keepdims=True) * (1.0 / (8 * rows))
    live = lax.broadcasted_iota(jnp.int32, centre.shape, 1) < count_ref[0]
    weight = jnp.where(live, 1.0 / (std[...] * scale), 0.0)
    spread = jnp.concatenate([(b[...] - centre) * weight for b in blocks], axis=0)
    misfit = jnp.where(live, (values[...] - own) / std[...] + noise[...], 0.0)
    gram_ref[...] = contract(spread[: 4 * rows], spread, ((1,), (1,)))
    cross_ref[...] = contract(misfit, spread, ((1,), (1,)))


def gram(count, blocks, noise, values, std, ens_scale):
    rows = blocks[0].shape[0]
    vmem = pl.BlockSpec(memory_space=pltpu.VMEM)
    return pl.pallas_call(
        lambda *refs: gram_kernel(ens_scale, *refs),
        in_specs=[pl.BlockSpec(memory_space=pltpu.SMEM)] + [vmem] * 11,
        out_specs=[vmem, vmem],
        out_shape=[
            jax.ShapeDtypeStruct((4 * rows, 8 * rows), F32),
            jax.ShapeDtypeStruct((rows, 8 * rows), F32),
        ],
        compiler_params=pltpu.CompilerParams(vmem_limit_bytes=32 << 20),
    )(count, *blocks, noise, values.reshape(1, -1), std.reshape(1, -1))


def spd_inverse(p):
    n = p.shape[0]
    row_id = lax.broadcasted_iota(jnp.int32, (n, n), 0)
    lane_id = lax.broadcasted_iota(jnp.int32, (1, n), 1)
    for i in range(0, n, 2):
        row0, row1 = p[i : i + 1], p[i + 1 : i + 2]
        col0 = jnp.broadcast_to(p[:, i : i + 1], (n, n))
        col1 = jnp.broadcast_to(p[:, i + 1 : i + 2], (n, n))
        a, b, c = col0[i : i + 1], col0[i + 1 : i + 2], col1[i + 1 : i + 2]
        r = 1.0 / (a * c - b * b)
        at0, at1 = lane_id == i, lane_id == i + 1
        in_pair = at0 | at1
        e0 = jnp.where(in_pair, jnp.where(at0, 1.0, 0.0), row0)
        e1 = jnp.where(in_pair, jnp.where(at1, 1.0, 0.0), row1)
        new0 = (c * r) * e0 - (b * r) * e1
        new1 = (a * r) * e1 - (b * r) * e0
        rest = jnp.where(in_pair, 0.0, p) - col0 * new0 - col1 * new1
        p = jnp.where(row_id == i, new0, jnp.where(row_id == i + 1, new1, rest))
    return p


def solve_kernel(scale, *refs):
    tops, bottoms, (other,) = refs[:4], refs[4:8], refs[8:9]
    blocks, (x_ref,) = refs[9:17], refs[17:]
    top = tops[0][...] + tops[1][...] + tops[2][...] + tops[3][...]
    bottom = bottoms[0][...] + bottoms[1][...] + bottoms[2][...] + bottoms[3][...]
    rows = jnp.concatenate([top, bottom], axis=0)
    n = rows.shape[0]
    eye = jnp.where(
        lax.broadcasted_iota(jnp.int32, (n, n), 0) == lax.broadcasted_iota(jnp.int32, (n, n), 1),
        1.0,
        0.0,
    )
    params = jnp.concatenate([b[...] for b in blocks], axis=0)
    anomaly = (params - jnp.sum(params, axis=0, keepdims=True) * (1.0 / (2 * n))) * (1.0 / scale)
    ff, fs = rows[:, :n] + eye, rows[:, n:]
    first = spd_inverse(ff)
    right = contract(first, jnp.concatenate([fs, anomaly[:n]], axis=1), ((1,), (0,)))
    down = contract(fs, right, ((0,), (0,)))
    second = spd_inverse(other[...] + eye - down[:, :n])
    x_second = contract(second, anomaly[n:] - down[:, n:], ((1,), (0,)))
    x_ref[:n] = right[:, n:] - contract(right[:, :n], x_second, ((1,), (0,)))
    x_ref[n:] = x_second


def solve(tops, bottoms, other, blocks, ens_scale):
    n = other.shape[0]
    vmem = pl.BlockSpec(memory_space=pltpu.VMEM)
    return pl.pallas_call(
        lambda *refs: solve_kernel(ens_scale, *refs),
        in_specs=[vmem] * 17,
        out_specs=vmem,
        out_shape=jax.ShapeDtypeStruct((2 * n, blocks[0].shape[1]), F32),
        compiler_params=pltpu.CompilerParams(vmem_limit_bytes=32 << 20),
        cost_estimate=pl.CostEstimate(
            flops=8 << 30, bytes_accessed=1 << 20, transcendentals=0
        ),
    )(*tops, *bottoms, other, *blocks)


def final_kernel(*refs):
    parts, (params, x_ref, out_ref) = refs[:4], refs[4:]
    cross = parts[0][...] + parts[1][...] + parts[2][...] + parts[3][...]
    out_ref[...] = params[...] + contract(cross, x_ref[...], ((1,), (0,)))


def final(parts, params, x):
    vmem = pl.BlockSpec(memory_space=pltpu.VMEM)
    return pl.pallas_call(
        final_kernel,
        in_specs=[vmem] * 6,
        out_specs=vmem,
        out_shape=jax.ShapeDtypeStruct(params.shape, F32),
    )(*parts, params, x)


def around_x(a):
    return [a] + [
        lax.ppermute(
            a, "space", [(z * 4 + x, z * 4 + (x + s) % 4) for z in range(4) for x in range(4)]
        )
        for s in (1, 3, 2)
    ]


def around_z(a):
    return [a] + [
        lax.ppermute(
            a, "space", [(z * 4 + x, (z + s) % 4 * 4 + x) for z in range(4) for x in range(4)]
        )
        for s in (1, 3, 2)
    ]


def around_y(a):
    return [a] + [
        lax.ppermute(a, "ens", [(e, (e + 2 * s) % 8) for e in range(8)]) for s in (1, 3, 2)
    ]


def partner(a):
    return lax.ppermute(a, "ens", [(e, e ^ 1) for e in range(8)])


def total4(parts):
    return (parts[0] + parts[1]) + (parts[2] + parts[3])


def shards(u, k, pos, count, values, std, noise, params):
    spaces = lax.axis_size("space")
    ens_scale = math.sqrt(u.shape[0] * lax.axis_size("ens") - 1.0)
    last = jnp.stack([u[:, -1], k[:, -1]])
    head = jnp.stack([u[:, 0], k[:, 0]])
    lo = lax.ppermute(last, "space", [(i, i + 1) for i in range(spaces - 1)])
    hi = lax.ppermute(head, "space", [(i + 1, i) for i in range(spaces - 1)])
    states, partial = stencil(pos, u, k)
    states, picked = faces(pos, u, k, lo, hi, states.reshape(u.shape), partial)

    mine = around_y(picked)
    blocks = mine + [partner(a) for a in mine]
    mine = around_y(params)
    param_blocks = mine + [partner(a) for a in mine]

    gram_rows, cross = gram(count, blocks, noise, values, std, ens_scale)
    n = gram_rows.shape[0]
    tops = around_z(total4(around_x(gram_rows[: n // 2])))
    bottoms = around_x(total4(around_z(gram_rows[n // 2 :])))
    square = jnp.concatenate([total4(tops)[:, :n], total4(bottoms)[:, :n]], axis=0)
    other = partner(square)
    crosses = around_z(total4(around_x(cross)))
    x = solve(tops, bottoms, other, param_blocks, ens_scale)
    return final(crosses, params, x), states


def solution(mesh):
    in_specs = (
        P("ens", "space", None, None),
        P("ens", "space", None, None),
        P("space"),
        P("space"),
        P("space"),
        P("space"),
        P("ens", "space"),
        P("ens", "space"),
    )
    out_specs = (P("ens", "space"), P("ens", "space", None, None))
    return jax.shard_map(shards, mesh=mesh, in_specs=in_specs, out_specs=out_specs, check_vma=False)
```

```python
import math

import jax
import jax.numpy as jnp
from jax import lax
from jax.experimental import pallas as pl
from jax.experimental.pallas import tpu as pltpu
from jax.sharding import PartitionSpec as P

step_size = 0.08
HIGH = lax.Precision.HIGHEST
F32 = jnp.float32


def shift_down(a, first):
    return jnp.concatenate([first, a[:-1]], axis=0)


def shift_up(a):
    return jnp.concatenate([a[1:], jnp.zeros_like(a[:1])], axis=0)


PAD = 8


def boundary(p, layers):
    z = p >> 13
    return (z == 0) | (z == layers - 1)


def sample_all(pos_ref, src_ref, dst_ref, list_ref, count_ref, stride, layers):
    members, slots = dst_ref.shape
    groups = members // 8
    lane = lax.broadcasted_iota(jnp.int32, (8, 128), 1)

    def block(jb, found):
        def chunk(jc, carry):
            found, accs = carry[0], list(carry[1:])
            for t in range(8):
                j = jc * 8 + t
                p = pos_ref[jb * 128 + j]
                list_ref[found] = jb * 128 + j
                found = found + boundary(p, layers).astype(jnp.int32)
                here = lane == j
                for g in range(groups):
                    v = src_ref[pl.ds(g * 8 * stride + (p >> 7), 8, stride=stride), :]
                    accs[g] = jnp.where(here, pltpu.roll(v, (j - p) & 127, 1), accs[g])
            return (found, *accs)

        start = (found,) + tuple(jnp.zeros((8, 128), F32) for _ in range(groups))
        found, *accs = lax.fori_loop(0, 16, chunk, start)
        at = pl.ds(pl.multiple_of(jb * 128, 128), 128)
        for g in range(groups):
            dst_ref[g * 8 : g * 8 + 8, at] = accs[g]
        return found

    count_ref[0] = lax.fori_loop(0, slots // 128, block, jnp.int32(0))


def sample_listed(pos_ref, list_ref, count_ref, src_ref, dst_ref, stride, nx):
    groups = dst_ref.shape[0] // 8
    lane = lax.broadcasted_iota(jnp.int32, (8, 128), 1)
    count, unroll = count_ref[0], 8

    def chunk(c, _):
        held = []
        for t in range(unroll):
            n = jnp.minimum(c * unroll + t, count - 1)
            j = list_ref[n]
            p = pos_ref[j]
            row = ((p >> 15) & 1) * nx + ((p >> 7) & (nx - 1))
            rolled = [
                pltpu.roll(
                    src_ref[pl.ds(g * 8 * stride + row, 8, stride=stride), :], (j - p) & 127, 1
                )
                for g in range(groups)
            ]
            held.append((j, rolled))
        for j, rolled in held:
            here = lane == (j & 127)
            at = pl.ds(pl.multiple_of((j >> 7) * 128, 128), 128)
            for g in range(groups):
                pltpu.store(dst_ref.at[g * 8 : g * 8 + 8, at], rolled[g], mask=here)
        return 0

    lax.fori_loop(0, (count + unroll - 1) // unroll, chunk, 0)


def stencil_kernel(
    pos_ref, u_ref, k_ref, out_ref, picked_ref, list_ref, count_ref, state, sem
):
    i = pl.program_id(0)
    members, layers, nx, ny = u_ref.shape
    lane = lax.broadcasted_iota(jnp.int32, (nx, ny), 1)
    first_lane, last_lane = lane == 0, lane == ny - 1
    half = step_size * 0.5

    def member(b, _):
        base = (i * members + b) * (layers * nx + PAD)
        u = u_ref[b, 0].astype(F32)
        k = k_ref[b, 0].astype(F32)
        below = None
        for z in range(layers):
            ku = k * u
            un = jnp.where(last_lane, 0.0, pltpu.roll(u, ny - 1, 1))
            kn = jnp.where(last_lane, 0.0, pltpu.roll(k, ny - 1, 1))
            f = (k + kn) * (un - u)
            acc = f - jnp.where(first_lane, ku, pltpu.roll(f, 1, 1))
            f = (k + shift_up(k)) * (shift_up(u) - u)
            acc = acc + (f - shift_down(f, ku[:1]))
            if below is not None:
                acc = acc - below
            u_now = u
            if z < layers - 1:
                u_next = u_ref[b, z + 1].astype(F32)
                k_next = k_ref[b, z + 1].astype(F32)
                below = (k + k_next) * (u_next - u)
                acc = acc + below
                u, k = u_next, k_next
            state[pl.ds(pl.multiple_of(base + z * nx, 8), nx), :] = u_now + half * acc
        return 0

    lax.fori_loop(0, members, member, 0)
    rows = layers * nx

    def push(m):
        return pltpu.make_async_copy(
            state.at[pl.ds(pl.multiple_of(m * (rows + PAD), 8), rows), :],
            out_ref.at[pl.ds(pl.multiple_of(m * rows, 8), rows), :],
            sem.at[m],
        )

    for b in range(members):
        push(i * members + b).start()

    @pl.when(i == pl.num_programs(0) - 1)
    def _():
        sample_all(pos_ref, state, picked_ref, list_ref, count_ref, rows + PAD, layers)
        for m in range(out_ref.shape[0] // rows):
            push(m).wait()


def stencil(pos, u, k):
    m, layers, nx, ny = u.shape
    per = 4
    block = pl.BlockSpec((per, layers, nx, ny), lambda i: (i, 0, 0, 0))
    rows = m * layers * nx
    return pl.pallas_call(
        stencil_kernel,
        grid=(m // per,),
        in_specs=[pl.BlockSpec(memory_space=pltpu.SMEM), block, block],
        out_specs=[
            pl.BlockSpec(memory_space=pl.ANY),
            pl.BlockSpec((m, pos.shape[0]), lambda i: (0, 0)),
            pl.BlockSpec(memory_space=pltpu.SMEM),
            pl.BlockSpec(memory_space=pltpu.SMEM),
        ],
        out_shape=[
            jax.ShapeDtypeStruct((rows, ny), F32),
            jax.ShapeDtypeStruct((m, pos.shape[0]), F32),
            jax.ShapeDtypeStruct((pos.shape[0] + 8,), jnp.int32),
            jax.ShapeDtypeStruct((1,), jnp.int32),
        ],
        scratch_shapes=[
            pltpu.VMEM((m * (layers * nx + PAD), ny), F32),
            pltpu.SemaphoreType.DMA((m,)),
        ],
        compiler_params=pltpu.CompilerParams(vmem_limit_bytes=32 << 20),
        cost_estimate=pl.CostEstimate(
            flops=40 * u.size, bytes_accessed=8 * u.size, transcendentals=0
        ),
    )(pos, u, k)


def faces_kernel(
    pos_ref, list_ref, count_ref, u_ref, k_ref, lo_ref, hi_ref, in_ref, partial_ref, params_ref, out_ref, picked_ref, extra, found
):
    g, side = pl.program_id(0), pl.program_id(1)
    members, _, nx, ny = u_ref.shape
    half = step_size * 0.5

    def apply(halo):
        def member(b, _):
            u = u_ref[b, 0].astype(F32)
            k = k_ref[b, 0].astype(F32)
            un = halo[0, b].astype(F32)
            kn = halo[1, b].astype(F32)
            d = half * ((k + kn) * (un - u))
            out_ref[b, 0] = in_ref[b, 0] + d
            at = (g * members + b) * (2 * nx + PAD) + side * nx
            extra[pl.ds(pl.multiple_of(at, 8), nx), :] = d
            return 0

        lax.fori_loop(0, members, member, 0)

    @pl.when(side == 0)
    def _():
        apply(lo_ref)

    @pl.when(side == 1)
    def _():
        apply(hi_ref)

    @pl.when((g == pl.num_programs(0) - 1) & (side == 1))
    def _():
        found[...] = jnp.zeros_like(found)
        sample_listed(pos_ref, list_ref, count_ref, extra, found, 2 * nx + PAD, nx)
        slots = found.shape[1]
        picked_ref[:, :slots] = partial_ref[...] + found[...]
        picked_ref[:, slots:] = params_ref[...]


def faces(pos, listed, count, u, k, lo, hi, states, partial, params):
    m, layers, nx, ny = u.shape
    per = 16
    face = pl.BlockSpec((per, 1, nx, ny), lambda g, s: (g, s * (layers - 1), 0, 0))
    halo = pl.BlockSpec((2, per, nx, ny), lambda g, s: (0, g, 0, 0))
    flat = pl.BlockSpec(partial.shape, lambda g, s: (0, 0))
    small = pl.BlockSpec(params.shape, lambda g, s: (0, 0))
    both = (m, partial.shape[1] + params.shape[1])
    return pl.pallas_call(
        faces_kernel,
        grid=(m // per, 2),
        in_specs=[pl.BlockSpec(memory_space=pltpu.SMEM)] * 3 + [face, face, halo, halo, face, flat, small],
        out_specs=[face, pl.BlockSpec(both, lambda g, s: (0, 0))],
        out_shape=[
            jax.ShapeDtypeStruct(states.shape, F32),
            jax.ShapeDtypeStruct(both, F32),
        ],
        scratch_shapes=[
            pltpu.VMEM((m * (2 * nx + PAD), ny), F32),
            pltpu.VMEM(partial.shape, F32),
        ],
        input_output_aliases={7: 0},
        compiler_params=pltpu.CompilerParams(vmem_limit_bytes=32 << 20),
        cost_estimate=pl.CostEstimate(
            flops=8 * m * nx * ny, bytes_accessed=24 * m * nx * ny, transcendentals=0
        ),
    )(pos, listed, count, u, k, lo, hi, states, partial, params)


def contract(a, b, dims):
    return lax.dot_general(a, b, (dims, ((), ())), precision=HIGH, preferred_element_type=F32)


def gram_kernel(scale, count_ref, core_ref, *refs):
    blocks, (noise, values, std, sum_ref) = refs[:8], refs[8:]
    rows = blocks[0].shape[0]
    n = 4 * rows
    slots = noise.shape[1]
    readings = [b[:, :slots] for b in blocks]
    own = readings[0]
    total = own
    for b in readings[1:]:
        total = total + b
    centre = jnp.sum(total, axis=0, keepdims=True) * (1.0 / (8 * rows))
    live = lax.broadcasted_iota(jnp.int32, centre.shape, 1) < count_ref[0]
    weight = jnp.where(live, 1.0 / (std[...] * scale), 0.0)
    first = jnp.concatenate([(b - centre) * weight for b in readings[:4]], axis=0)
    second = jnp.concatenate([(b - centre) * weight for b in readings[4:]], axis=0)
    misfit = jnp.where(live, (values[...] - own) / std[...] + noise[...], 0.0)
    on_first = contract(
        jnp.concatenate([first, second[: n // 2], misfit], axis=0), first, ((1,), (1,))
    )
    on_second = contract(
        jnp.concatenate([first[n // 2 :], misfit], axis=0), second, ((1,), (1,))
    )
    is_first = core_ref[0] == 0
    sum_ref[:n] = on_first[:n]
    sum_ref[n : n + n // 2] = jnp.where(is_first, on_first[n : n + n // 2], on_second[: n // 2])
    sum_ref[n + n // 2 : n + n // 2 + rows] = on_first[n + n // 2 :]
    sum_ref[n + n // 2 + rows :] = on_second[n // 2 :]


def gram(count, core, blocks, noise, values, std, ens_scale):
    rows = blocks[0].shape[0]
    vmem = pl.BlockSpec(memory_space=pltpu.VMEM)
    return pl.pallas_call(
        lambda *refs: gram_kernel(ens_scale, *refs),
        in_specs=[pl.BlockSpec(memory_space=pltpu.SMEM)] * 2 + [vmem] * 11,
        out_specs=vmem,
        out_shape=jax.ShapeDtypeStruct((8 * rows, 4 * rows), F32),
        compiler_params=pltpu.CompilerParams(vmem_limit_bytes=16 << 20),
    )(count, core, *blocks, noise, values.reshape(1, -1), std.reshape(1, -1))


def inverse4(k):
    r = 1.0 / (k[0][0] * k[1][1] - k[0][1] * k[0][1])
    a00, a01, a11 = k[1][1] * r, -k[0][1] * r, k[0][0] * r
    t00, t01 = a00 * k[0][2] + a01 * k[1][2], a00 * k[0][3] + a01 * k[1][3]
    t10, t11 = a01 * k[0][2] + a11 * k[1][2], a01 * k[0][3] + a11 * k[1][3]
    s00 = k[2][2] - (k[0][2] * t00 + k[1][2] * t10)
    s01 = k[2][3] - (k[0][2] * t01 + k[1][2] * t11)
    s11 = k[3][3] - (k[0][3] * t01 + k[1][3] * t11)
    q = 1.0 / (s00 * s11 - s01 * s01)
    i00, i01, i11 = s11 * q, -s01 * q, s00 * q
    v00, v01 = t00 * i00 + t01 * i01, t00 * i01 + t01 * i11
    v10, v11 = t10 * i00 + t11 * i01, t10 * i01 + t11 * i11
    b00 = a00 + v00 * t00 + v01 * t01
    b01 = a01 + v00 * t10 + v01 * t11
    b11 = a11 + v10 * t10 + v11 * t11
    return [
        [b00, b01, -v00, -v01],
        [b01, b11, -v10, -v11],
        [-v00, -v10, i00, i01],
        [-v01, -v11, i01, i11],
    ]


def pivoted_inverse(p):
    n = p.shape[0]
    tiles = [p[t : t + 8] for t in range(0, n, 8)]
    row = lax.broadcasted_iota(jnp.int32, (8, n), 0)
    lane = lax.broadcasted_iota(jnp.int32, (8, n), 1)
    lane1 = lax.broadcasted_iota(jnp.int32, (1, n), 1)

    def spread(tile, at):
        return jnp.broadcast_to(tile[:, at : at + 1], (8, n))

    def entries(tile, at):
        columns = [spread(tile, at + b) for b in range(4)]
        return [[columns[b][at % 8 + a : at % 8 + a + 1] for b in range(4)] for a in range(4)]

    def dot4(x, y):
        return (x[0] * y[0] + x[1] * y[1]) + (x[2] * y[2] + x[3] * y[3])

    inv = inverse4(entries(tiles[0], 0))
    for i in range(0, n, 4):
        here, off = i // 8, i % 8
        cols = [[spread(t, i + b) for t in tiles] for b in range(4)]
        ahead = None
        if i + 4 < n:
            there, shift = (i + 4) // 8, (i + 4) % 8
            q = entries(tiles[there], i + 4)
            c = [[cols[m][there][shift + a : shift + a + 1] for m in range(4)] for a in range(4)]
            w = [[dot4(inv[m], c[b]) for m in range(4)] for b in range(4)]
            ahead = inverse4(
                [[q[a][b] - dot4(c[a], w[b]) if a <= b else None for b in range(4)] for a in range(4)]
            )
        inside1 = (lane1 >= i) & (lane1 < i + 4)
        e = [
            jnp.where(
                inside1, jnp.where(lane1 == i + a, 1.0, 0.0), tiles[here][off + a : off + a + 1]
            )
            for a in range(4)
        ]
        new = [dot4(inv[a], e) for a in range(4)]
        inside = (lane >= i) & (lane < i + 4)
        for t in range(n // 8):
            rest = jnp.where(inside, 0.0, tiles[t])
            tiles[t] = rest - (
                (cols[0][t] * new[0] + cols[1][t] * new[1])
                + (cols[2][t] * new[2] + cols[3][t] * new[3])
            )
        for a in range(4):
            tiles[here] = jnp.where(row == off + a, new[a], tiles[here])
        inv = ahead
    return jnp.concatenate(tiles, axis=0)


def spd_inverse(p):
    n = p.shape[0]
    if n <= 64:
        return pivoted_inverse(p)
    h = n // 2
    corner, side = p[:h, :h], p[:h, h:]
    first = spd_inverse(corner)
    ahead = contract(first, side, ((1,), (0,)))
    second = spd_inverse(p[h:, h:] - contract(side, ahead, ((0,), (0,))))
    mixed = contract(ahead, second, ((1,), (0,)))
    top = jnp.concatenate([first + contract(mixed, ahead, ((1,), (1,))), -mixed], axis=1)
    return jnp.concatenate([top, jnp.concatenate([-mixed.T, second], axis=1)], axis=0)


def identity(n):
    return jnp.where(
        lax.broadcasted_iota(jnp.int32, (n, n), 0) == lax.broadcasted_iota(jnp.int32, (n, n), 1),
        1.0,
        0.0,
    )


def inverse_kernel(sum_ref, out_ref):
    n = out_ref.shape[0]
    out_ref[...] = spd_inverse(sum_ref[:n] + identity(n))


def inverse(sums):
    n = sums.shape[1]
    vmem = pl.BlockSpec(memory_space=pltpu.VMEM)
    return pl.pallas_call(
        inverse_kernel,
        in_specs=[vmem],
        out_specs=vmem,
        out_shape=jax.ShapeDtypeStruct((n, n), F32),
        compiler_params=pltpu.CompilerParams(vmem_limit_bytes=4 << 20),
        cost_estimate=pl.CostEstimate(flops=4 << 30, bytes_accessed=1 << 20, transcendentals=0),
    )(sums)


def update_kernel(scale, core_ref, inv_ref, sum_ref, other_ref, *refs):
    blocks, out_ref = refs[:8], refs[8]
    n = inv_ref.shape[0]
    half, rows = n // 2, blocks[0].shape[0]
    width = out_ref.shape[1]
    params = jnp.concatenate([b[:, -width:] for b in blocks], axis=0)
    anomaly = (params - jnp.sum(params, axis=0, keepdims=True) * (1.0 / (2 * n))) * (1.0 / scale)
    is_first = core_ref[0] == 0
    mine, theirs = sum_ref[n : n + half], other_ref[n : n + half]
    product = jnp.concatenate(
        [jnp.where(is_first, mine, theirs), jnp.where(is_first, theirs, mine)], axis=0
    )
    fs = jnp.where(is_first, product.T, product)
    right = contract(inv_ref[...], jnp.concatenate([fs, anomaly[:n]], axis=1), ((1,), (0,)))
    down = contract(fs, right, ((0,), (0,)))
    second = spd_inverse(other_ref[:n] + identity(n) - down[:, :n])
    x_second = contract(second, anomaly[n:] - down[:, n:], ((1,), (0,)))
    x_first = right[:, n:] - contract(right[:, :n], x_second, ((1,), (0,)))
    cross_first, cross_second = sum_ref[n + half : n + half + rows], sum_ref[n + half + rows :]
    out_ref[...] = params[:rows] + (
        contract(cross_first, x_first, ((1,), (0,))) + contract(cross_second, x_second, ((1,), (0,)))
    )


def update(core, inv, sums, other, blocks, width, ens_scale):
    vmem = pl.BlockSpec(memory_space=pltpu.VMEM)
    return pl.pallas_call(
        lambda *refs: update_kernel(ens_scale, *refs),
        in_specs=[pl.BlockSpec(memory_space=pltpu.SMEM)] + [vmem] * 11,
        out_specs=vmem,
        out_shape=jax.ShapeDtypeStruct((blocks[0].shape[0], width), F32),
        compiler_params=pltpu.CompilerParams(vmem_limit_bytes=16 << 20),
    )(core, inv, sums, other, *blocks)


def around_x(a):
    return [a] + [
        lax.ppermute(
            a, "space", [(z * 4 + x, z * 4 + (x + s) % 4) for z in range(4) for x in range(4)]
        )
        for s in (1, 3, 2)
    ]


def around_z(a):
    return [a] + [
        lax.ppermute(
            a, "space", [(z * 4 + x, (z + s) % 4 * 4 + x) for z in range(4) for x in range(4)]
        )
        for s in (1, 3, 2)
    ]


def around_y(a):
    return [a] + [
        lax.ppermute(a, "ens", [(e, (e + 2 * s) % 8) for e in range(8)]) for s in (1, 3, 2)
    ]


def partner(a):
    return lax.ppermute(a, "ens", [(e, e ^ 1) for e in range(8)])


def total4(parts):
    return (parts[0] + parts[1]) + (parts[2] + parts[3])


def shards(u, k, pos, count, values, std, noise, params):
    spaces = lax.axis_size("space")
    ens_scale = math.sqrt(u.shape[0] * lax.axis_size("ens") - 1.0)
    last = jnp.stack([u[:, -1], k[:, -1]])
    head = jnp.stack([u[:, 0], k[:, 0]])
    lo = lax.ppermute(last, "space", [(i, i + 1) for i in range(spaces - 1)])
    hi = lax.ppermute(head, "space", [(i + 1, i) for i in range(spaces - 1)])
    states, partial, listed, found = stencil(pos, u, k)
    states, picked = faces(
        pos, listed, found, u, k, lo, hi, states.reshape(u.shape), partial, params
    )

    mine = around_y(picked)
    blocks = mine + [partner(a) for a in mine]

    core = (lax.axis_index("ens") % 2).astype(jnp.int32).reshape(1)
    sums = gram(count, core, blocks, noise, values, std, ens_scale)
    sums = total4(around_z(total4(around_x(sums))))
    other = partner(sums)
    inv = inverse(sums)
    return update(core, inv, sums, other, blocks, params.shape[1], ens_scale), states


def solution(mesh):
    in_specs = (
        P("ens", "space", None, None),
        P("ens", "space", None, None),
        P("space"),
        P("space"),
        P("space"),
        P("space"),
        P("ens", "space"),
        P("ens", "space"),
    )
    out_specs = (P("ens", "space"), P("ens", "space", None, None))
    return jax.shard_map(shards, mesh=mesh, in_specs=in_specs, out_specs=out_specs, check_vma=False)
```

```python
import math

import jax
import jax.numpy as jnp
from jax import lax
from jax.experimental import pallas as pl
from jax.experimental.pallas import tpu as pltpu
from jax.sharding import PartitionSpec as P

step_size = 0.08
HIGH = lax.Precision.HIGHEST
F32 = jnp.float32


def shift_down(a, first):
    return jnp.concatenate([first, a[:-1]], axis=0)


def shift_up(a):
    return jnp.concatenate([a[1:], jnp.zeros_like(a[:1])], axis=0)


GROUP = 8


def set_lanes(pos, lanes, layers, nx, ny):
    slots = lanes.shape[1]
    lane = lax.broadcasted_iota(jnp.int32, (ny, slots), 0)
    for section, layer in enumerate(layers):
        own = jnp.where(pos // (nx * ny) == layer, pos % ny, -1)
        hot = jnp.where(lane == own, 1.0, 0.0).astype(jnp.bfloat16)
        base = 2 * section * ny
        lanes[base : base + ny] = hot
        lanes[base + ny : base + 2 * ny] = hot


def put(pair, rows, section, value):
    ny = value.shape[1]
    high = value.astype(jnp.bfloat16)
    base = 2 * section * ny
    pair[rows, base : base + ny] = high
    pair[rows, base + ny : base + 2 * ny] = (value - high.astype(F32)).astype(jnp.bfloat16)


def pick(pair, lanes, x, sums, base, nx, chunk=256):
    slots = lanes.shape[1]
    row = lax.broadcasted_iota(jnp.int32, (nx, chunk), 0)
    for c in range(0, slots, chunk):
        t = jnp.dot(pair[...], lanes[:, c : c + chunk], preferred_element_type=F32)
        hit = row == x[:, c : c + chunk]
        for b in range(GROUP):
            part = jnp.where(hit, t[b * nx : (b + 1) * nx], 0.0)
            at = pl.ds(pl.multiple_of(base + b * 8, 8), 8)
            sums[at, c : c + chunk] = jnp.sum(part.reshape(nx // 8, 8, chunk), axis=0)


def add_eights(sums):
    m = sums.shape[0] // 8
    member = lax.broadcasted_iota(jnp.int32, (m, 8 * m), 1) // 8
    add = jnp.where(member == lax.broadcasted_iota(jnp.int32, (m, 8 * m), 0), 1.0, 0.0)
    return contract(add, sums, ((1,), (0,)))


def stencil_kernel(pos_ref, u_ref, k_ref, out_ref, picked_ref, lanes, pair, sums):
    i = pl.program_id(0)
    members, layers, nx, ny = u_ref.shape
    lane = lax.broadcasted_iota(jnp.int32, (nx, ny), 1)
    first_lane, last_lane = lane == 0, lane == ny - 1
    half = step_size * 0.5

    @pl.when(i == 0)
    def _():
        set_lanes(pos_ref[...], lanes, range(layers), nx, ny)

    def member(b, _):
        u = u_ref[b, 0].astype(F32)
        k = k_ref[b, 0].astype(F32)
        below = None
        for z in range(layers):
            ku = k * u
            un = jnp.where(last_lane, 0.0, pltpu.roll(u, ny - 1, 1))
            kn = jnp.where(last_lane, 0.0, pltpu.roll(k, ny - 1, 1))
            f = (k + kn) * (un - u)
            acc = f - jnp.where(first_lane, ku, pltpu.roll(f, 1, 1))
            f = (k + shift_up(k)) * (shift_up(u) - u)
            acc = acc + (f - shift_down(f, ku[:1]))
            if below is not None:
                acc = acc - below
            u_now = u
            if z < layers - 1:
                u_next = u_ref[b, z + 1].astype(F32)
                k_next = k_ref[b, z + 1].astype(F32)
                below = (k + k_next) * (u_next - u)
                acc = acc + below
                u, k = u_next, k_next
            value = u_now + half * acc
            out_ref[b, z] = value
            put(pair, pl.ds(pl.multiple_of(b * nx, nx), nx), z, value)
        return 0

    lax.fori_loop(0, members, member, 0)
    pick(pair, lanes, pos_ref[...] // ny % nx, sums, i * members * 8, nx)

    @pl.when(i == pl.num_programs(0) - 1)
    def _():
        picked_ref[...] = add_eights(sums[...])


def stencil(pos, u, k):
    m, layers, nx, ny = u.shape
    per = GROUP
    block = pl.BlockSpec((per, layers, nx, ny), lambda i: (i, 0, 0, 0))
    slots = pos.shape[1]
    return pl.pallas_call(
        stencil_kernel,
        grid=(m // per,),
        in_specs=[pl.BlockSpec(pos.shape, lambda i: (0, 0)), block, block],
        out_specs=[block, pl.BlockSpec((m, slots), lambda i: (0, 0))],
        out_shape=[
            jax.ShapeDtypeStruct(u.shape, F32),
            jax.ShapeDtypeStruct((m, slots), F32),
        ],
        scratch_shapes=[
            pltpu.VMEM((2 * layers * ny, slots), jnp.bfloat16),
            pltpu.VMEM((per * nx, 2 * layers * ny), jnp.bfloat16),
            pltpu.VMEM((8 * m, slots), F32),
        ],
        compiler_params=pltpu.CompilerParams(vmem_limit_bytes=24 << 20),
        cost_estimate=pl.CostEstimate(
            flops=40 * u.size, bytes_accessed=8 * u.size, transcendentals=0
        ),
    )(pos, u, k)


def face_flux(own, halo, b):
    u, k = own[0, b].astype(F32), own[1, b].astype(F32)
    return (step_size * 0.5) * ((k + halo[1, b].astype(F32)) * (halo[0, b].astype(F32) - u))


def readings_kernel(
    last_layer, pos_ref, head_ref, last_ref, lo_ref, hi_ref, partial_ref, params_ref, out_ref,
    lanes, pair, sums
):
    _, members, nx, ny = head_ref.shape
    slots = partial_ref.shape[1]
    set_lanes(pos_ref[...], lanes, (0, last_layer), nx, ny)
    x = pos_ref[...] // ny % nx

    def group(q, _):
        def member(b, _):
            rows = pl.ds(pl.multiple_of(b * nx, nx), nx)
            put(pair, rows, 0, face_flux(head_ref, lo_ref, q * GROUP + b))
            put(pair, rows, 1, face_flux(last_ref, hi_ref, q * GROUP + b))
            return 0

        lax.fori_loop(0, GROUP, member, 0, unroll=2)
        pick(pair, lanes, x, sums, q * GROUP * 8, nx)
        return 0

    lax.fori_loop(0, members // GROUP, group, 0)
    out_ref[:, :slots] = partial_ref[...] + add_eights(sums[...])
    out_ref[:, slots:] = params_ref[...]


def readings(pos, head, last, lo, hi, partial, params, layers):
    _, m, nx, ny = head.shape
    slots = pos.shape[1]
    vmem = pl.BlockSpec(memory_space=pltpu.VMEM)
    return pl.pallas_call(
        lambda *refs: readings_kernel(layers - 1, *refs),
        in_specs=[vmem] * 7,
        out_specs=vmem,
        out_shape=jax.ShapeDtypeStruct((m, slots + params.shape[1]), F32),
        scratch_shapes=[
            pltpu.VMEM((4 * ny, slots), jnp.bfloat16),
            pltpu.VMEM((GROUP * nx, 4 * ny), jnp.bfloat16),
            pltpu.VMEM((8 * m, slots), F32),
        ],
        compiler_params=pltpu.CompilerParams(vmem_limit_bytes=8 << 20),
        cost_estimate=pl.CostEstimate(
            flops=8 * m * nx * ny, bytes_accessed=8 << 20, transcendentals=0
        ),
    )(pos, head, last, lo, hi, partial, params)


def faces_kernel(u_ref, k_ref, lo_ref, hi_ref, in_ref, out_ref):
    side = pl.program_id(1)

    def apply(halo):
        def member(b, _):
            u, k = u_ref[b, 0].astype(F32), k_ref[b, 0].astype(F32)
            flux = (k + halo[1, b].astype(F32)) * (halo[0, b].astype(F32) - u)
            out_ref[b, 0] = in_ref[b, 0] + (step_size * 0.5) * flux
            return 0

        lax.fori_loop(0, in_ref.shape[0], member, 0)

    @pl.when(side == 0)
    def _():
        apply(lo_ref)

    @pl.when(side == 1)
    def _():
        apply(hi_ref)


def faces(u, k, lo, hi, states):
    m, layers, nx, ny = states.shape
    per = 16
    face = pl.BlockSpec((per, 1, nx, ny), lambda g, s: (g, s * (layers - 1), 0, 0))
    halo = pl.BlockSpec((2, per, nx, ny), lambda g, s: (0, g, 0, 0))
    return pl.pallas_call(
        faces_kernel,
        grid=(m // per, 2),
        in_specs=[face, face, halo, halo, face],
        out_specs=face,
        out_shape=jax.ShapeDtypeStruct(states.shape, F32),
        input_output_aliases={4: 0},
        compiler_params=pltpu.CompilerParams(vmem_limit_bytes=58 << 20),
        cost_estimate=pl.CostEstimate(
            flops=8 * m * nx * ny, bytes_accessed=24 * m * nx * ny, transcendentals=0
        ),
    )(u, k, lo, hi, states)


def contract(a, b, dims):
    return lax.dot_general(a, b, (dims, ((), ())), precision=HIGH, preferred_element_type=F32)


def gram_kernel(scale, count_ref, core_ref, *refs):
    blocks, (noise, values, std, sum_ref, anomaly_ref) = refs[:8], refs[8:]
    rows = blocks[0].shape[0]
    n = 4 * rows
    slots = noise.shape[1]
    readings = [b[:, :slots] for b in blocks]
    own = readings[0]
    total = own
    for b in readings[1:]:
        total = total + b
    centre = jnp.sum(total, axis=0, keepdims=True) * (1.0 / (8 * rows))
    live = lax.broadcasted_iota(jnp.int32, centre.shape, 1) < count_ref[0]
    weight = jnp.where(live, 1.0 / (std[...] * scale), 0.0)
    first = jnp.concatenate([(b - centre) * weight for b in readings[:4]], axis=0)
    second = jnp.concatenate([(b - centre) * weight for b in readings[4:]], axis=0)
    misfit = jnp.where(live, (values[...] - own) / std[...] + noise[...], 0.0)
    on_first = contract(
        jnp.concatenate([first, second[: n // 2], misfit], axis=0), first, ((1,), (1,))
    )
    on_second = contract(
        jnp.concatenate([first[n // 2 :], misfit], axis=0), second, ((1,), (1,))
    )
    params = jnp.concatenate([b[:, slots:] for b in blocks], axis=0)
    mean = jnp.sum(params, axis=0, keepdims=True) * (1.0 / (2 * n))
    anomaly_ref[...] = (params - mean) * (1.0 / scale)
    is_first = core_ref[0] == 0
    sum_ref[:n] = on_first[:n]
    sum_ref[n : n + n // 2] = jnp.where(is_first, on_first[n : n + n // 2], on_second[: n // 2])
    sum_ref[n + n // 2 : n + n // 2 + rows] = on_first[n + n // 2 :]
    sum_ref[n + n // 2 + rows :] = on_second[n // 2 :]


def gram(count, core, blocks, noise, values, std, ens_scale):
    rows = blocks[0].shape[0]
    vmem = pl.BlockSpec(memory_space=pltpu.VMEM)
    return pl.pallas_call(
        lambda *refs: gram_kernel(ens_scale, *refs),
        in_specs=[pl.BlockSpec(memory_space=pltpu.SMEM)] * 2 + [vmem] * 11,
        out_specs=[vmem, vmem],
        out_shape=[
            jax.ShapeDtypeStruct((8 * rows, 4 * rows), F32),
            jax.ShapeDtypeStruct((8 * rows, blocks[0].shape[1] - noise.shape[1]), F32),
        ],
        compiler_params=pltpu.CompilerParams(vmem_limit_bytes=16 << 20),
    )(count, core, *blocks, noise, values.reshape(1, -1), std.reshape(1, -1))


def inverse4(k):
    r = 1.0 / (k[0][0] * k[1][1] - k[0][1] * k[0][1])
    a00, a01, a11 = k[1][1] * r, -k[0][1] * r, k[0][0] * r
    t00, t01 = a00 * k[0][2] + a01 * k[1][2], a00 * k[0][3] + a01 * k[1][3]
    t10, t11 = a01 * k[0][2] + a11 * k[1][2], a01 * k[0][3] + a11 * k[1][3]
    s00 = k[2][2] - (k[0][2] * t00 + k[1][2] * t10)
    s01 = k[2][3] - (k[0][2] * t01 + k[1][2] * t11)
    s11 = k[3][3] - (k[0][3] * t01 + k[1][3] * t11)
    q = 1.0 / (s00 * s11 - s01 * s01)
    i00, i01, i11 = s11 * q, -s01 * q, s00 * q
    v00, v01 = t00 * i00 + t01 * i01, t00 * i01 + t01 * i11
    v10, v11 = t10 * i00 + t11 * i01, t10 * i01 + t11 * i11
    b00 = a00 + v00 * t00 + v01 * t01
    b01 = a01 + v00 * t10 + v01 * t11
    b11 = a11 + v10 * t10 + v11 * t11
    return [
        [b00, b01, -v00, -v01],
        [b01, b11, -v10, -v11],
        [-v00, -v10, i00, i01],
        [-v01, -v11, i01, i11],
    ]


def pivoted_inverse(p):
    n = p.shape[0]
    tiles = [p[t : t + 8] for t in range(0, n, 8)]
    row = lax.broadcasted_iota(jnp.int32, (8, n), 0)
    lane = lax.broadcasted_iota(jnp.int32, (8, n), 1)
    lane1 = lax.broadcasted_iota(jnp.int32, (1, n), 1)

    def spread(tile, at):
        return jnp.broadcast_to(tile[:, at : at + 1], (8, n))

    def entries(tile, at):
        columns = [spread(tile, at + b) for b in range(4)]
        return [[columns[b][at % 8 + a : at % 8 + a + 1] for b in range(4)] for a in range(4)]

    def dot4(x, y):
        return (x[0] * y[0] + x[1] * y[1]) + (x[2] * y[2] + x[3] * y[3])

    inv = inverse4(entries(tiles[0], 0))
    for i in range(0, n, 4):
        here, off = i // 8, i % 8
        cols = [[spread(t, i + b) for t in tiles] for b in range(4)]
        ahead = None
        if i + 4 < n:
            there, shift = (i + 4) // 8, (i + 4) % 8
            q = entries(tiles[there], i + 4)
            c = [[cols[m][there][shift + a : shift + a + 1] for m in range(4)] for a in range(4)]
            w = [[dot4(inv[m], c[b]) for m in range(4)] for b in range(4)]
            ahead = inverse4(
                [[q[a][b] - dot4(c[a], w[b]) if a <= b else None for b in range(4)] for a in range(4)]
            )
        inside1 = (lane1 >= i) & (lane1 < i + 4)
        e = [
            jnp.where(
                inside1, jnp.where(lane1 == i + a, 1.0, 0.0), tiles[here][off + a : off + a + 1]
            )
            for a in range(4)
        ]
        new = [dot4(inv[a], e) for a in range(4)]
        inside = (lane >= i) & (lane < i + 4)
        for t in range(n // 8):
            rest = jnp.where(inside, 0.0, tiles[t])
            tiles[t] = rest - (
                (cols[0][t] * new[0] + cols[1][t] * new[1])
                + (cols[2][t] * new[2] + cols[3][t] * new[3])
            )
        for a in range(4):
            tiles[here] = jnp.where(row == off + a, new[a], tiles[here])
        inv = ahead
    return jnp.concatenate(tiles, axis=0)


def spd_inverse(p):
    n = p.shape[0]
    if n <= 64:
        return pivoted_inverse(p)
    h = n // 2
    corner, side = p[:h, :h], p[:h, h:]
    first = spd_inverse(corner)
    ahead = contract(first, side, ((1,), (0,)))
    second = spd_inverse(p[h:, h:] - contract(side, ahead, ((0,), (0,))))
    mixed = contract(ahead, second, ((1,), (0,)))
    top = jnp.concatenate([first + contract(mixed, ahead, ((1,), (1,))), -mixed], axis=1)
    return jnp.concatenate([top, jnp.concatenate([-mixed.T, second], axis=1)], axis=0)


def identity(n):
    return jnp.where(
        lax.broadcasted_iota(jnp.int32, (n, n), 0) == lax.broadcasted_iota(jnp.int32, (n, n), 1),
        1.0,
        0.0,
    )


def inverse_kernel(sum_ref, out_ref):
    n = out_ref.shape[0]
    out_ref[...] = spd_inverse(sum_ref[:n] + identity(n))


def inverse(sums):
    n = sums.shape[1]
    vmem = pl.BlockSpec(memory_space=pltpu.VMEM)
    return pl.pallas_call(
        inverse_kernel,
        in_specs=[vmem],
        out_specs=vmem,
        out_shape=jax.ShapeDtypeStruct((n, n), F32),
        compiler_params=pltpu.CompilerParams(vmem_limit_bytes=4 << 20),
        cost_estimate=pl.CostEstimate(flops=4 << 30, bytes_accessed=1 << 20, transcendentals=0),
    )(sums)


def update_kernel(core_ref, inv_ref, sum_ref, other_ref, anomaly_ref, params_ref, out_ref):
    n = inv_ref.shape[0]
    half, rows = n // 2, params_ref.shape[0]
    anomaly = anomaly_ref[...]
    is_first = core_ref[0] == 0
    mine, theirs = sum_ref[n : n + half], other_ref[n : n + half]
    product = jnp.concatenate(
        [jnp.where(is_first, mine, theirs), jnp.where(is_first, theirs, mine)], axis=0
    )
    fs = jnp.where(is_first, product.T, product)
    right = contract(inv_ref[...], jnp.concatenate([fs, anomaly[:n]], axis=1), ((1,), (0,)))
    down = contract(fs, right, ((0,), (0,)))
    second = spd_inverse(other_ref[:n] + identity(n) - down[:, :n])
    x_second = contract(second, anomaly[n:] - down[:, n:], ((1,), (0,)))
    x_first = right[:, n:] - contract(right[:, :n], x_second, ((1,), (0,)))
    cross_first, cross_second = sum_ref[n + half : n + half + rows], sum_ref[n + half + rows :]
    out_ref[...] = params_ref[...] + (
        contract(cross_first, x_first, ((1,), (0,))) + contract(cross_second, x_second, ((1,), (0,)))
    )


def update(core, inv, sums, other, anomaly, params):
    vmem = pl.BlockSpec(memory_space=pltpu.VMEM)
    return pl.pallas_call(
        update_kernel,
        in_specs=[pl.BlockSpec(memory_space=pltpu.SMEM)] + [vmem] * 5,
        out_specs=vmem,
        out_shape=jax.ShapeDtypeStruct(params.shape, F32),
        compiler_params=pltpu.CompilerParams(vmem_limit_bytes=8 << 20),
    )(core, inv, sums, other, anomaly, params)


def around_x(a):
    return [a] + [
        lax.ppermute(
            a, "space", [(z * 4 + x, z * 4 + (x + s) % 4) for z in range(4) for x in range(4)]
        )
        for s in (1, 3, 2)
    ]


def around_z(a):
    return [a] + [
        lax.ppermute(
            a, "space", [(z * 4 + x, (z + s) % 4 * 4 + x) for z in range(4) for x in range(4)]
        )
        for s in (1, 3, 2)
    ]


def around_y(a):
    return [a] + [
        lax.ppermute(a, "ens", [(e, (e + 2 * s) % 8) for e in range(8)]) for s in (1, 3, 2)
    ]


def partner(a):
    return lax.ppermute(a, "ens", [(e, e ^ 1) for e in range(8)])


def total4(parts):
    return (parts[0] + parts[1]) + (parts[2] + parts[3])


def shards(u, k, pos, count, values, std, noise, params):
    spaces = lax.axis_size("space")
    ens_scale = math.sqrt(u.shape[0] * lax.axis_size("ens") - 1.0)
    last = jnp.stack([u[:, -1], k[:, -1]])
    head = jnp.stack([u[:, 0], k[:, 0]])
    lo = lax.ppermute(last, "space", [(i, i + 1) for i in range(spaces - 1)])
    hi = lax.ppermute(head, "space", [(i + 1, i) for i in range(spaces - 1)])
    cells = pos.reshape(1, -1)
    states, partial = stencil(cells, u, k)
    picked = readings(cells, head, last, lo, hi, partial, params, u.shape[1])
    mine = around_y(picked)
    blocks = mine + [partner(a) for a in mine]

    core = (lax.axis_index("ens") % 2).astype(jnp.int32).reshape(1)
    sums, anomaly = gram(count, core, blocks, noise, values, std, ens_scale)
    lo, hi, sums = lax.optimization_barrier((lo, hi, sums))
    states = faces(u, k, lo, hi, states)
    sums, states = lax.optimization_barrier((total4(around_x(sums)), states))
    sums = total4(around_z(sums))
    other = partner(sums)
    inv = inverse(sums)
    return update(core, inv, sums, other, anomaly, params), states


def solution(mesh):
    in_specs = (
        P("ens", "space", None, None),
        P("ens", "space", None, None),
        P("space"),
        P("space"),
        P("space"),
        P("space"),
        P("ens", "space"),
        P("ens", "space"),
    )
    out_specs = (P("ens", "space"), P("ens", "space", None, None))
    return jax.shard_map(shards, mesh=mesh, in_specs=in_specs, out_specs=out_specs, check_vma=False)
```

```python
import math

import jax
import jax.numpy as jnp
from jax import lax
from jax.experimental import pallas as pl
from jax.experimental.pallas import tpu as pltpu
from jax.sharding import PartitionSpec as P

step_size = 0.08
HIGH = lax.Precision.HIGHEST
F32 = jnp.float32


def shift_down(a, first):
    return jnp.concatenate([first, a[:-1]], axis=0)


def shift_up(a):
    return jnp.concatenate([a[1:], jnp.zeros_like(a[:1])], axis=0)


GROUP = 8


def set_lanes(pos, lanes, layers, nx, ny):
    slots = lanes.shape[1]
    lane = lax.broadcasted_iota(jnp.int32, (ny, slots), 0)
    for section, layer in enumerate(layers):
        own = jnp.where(pos // (nx * ny) == layer, pos % ny, -1)
        hot = jnp.where(lane == own, 1.0, 0.0).astype(jnp.bfloat16)
        base = 2 * section * ny
        lanes[base : base + ny] = hot
        lanes[base + ny : base + 2 * ny] = hot


def put(pair, rows, section, value):
    ny = value.shape[1]
    high = value.astype(jnp.bfloat16)
    base = 2 * section * ny
    pair[rows, base : base + ny] = high
    pair[rows, base + ny : base + 2 * ny] = (value - high.astype(F32)).astype(jnp.bfloat16)


def pick(pair, lanes, x, sums, base, nx, chunk=256):
    slots = lanes.shape[1]
    row = lax.broadcasted_iota(jnp.int32, (nx, chunk), 0)
    for c in range(0, slots, chunk):
        t = jnp.dot(pair[...], lanes[:, c : c + chunk], preferred_element_type=F32)
        hit = row == x[:, c : c + chunk]
        for b in range(pair.shape[0] // nx):
            part = jnp.where(hit, t[b * nx : (b + 1) * nx], 0.0)
            at = pl.ds(pl.multiple_of(base + b * 8, 8), 8)
            sums[at, c : c + chunk] = jnp.sum(part.reshape(nx // 8, 8, chunk), axis=0)


def add_eights(sums):
    m = sums.shape[0] // 8
    member = lax.broadcasted_iota(jnp.int32, (m, 8 * m), 1) // 8
    add = jnp.where(member == lax.broadcasted_iota(jnp.int32, (m, 8 * m), 0), 1.0, 0.0)
    return contract(add, sums, ((1,), (0,)))


def stencil_kernel(pos_ref, u_ref, k_ref, out_ref, picked_ref, lanes, pair, sums):
    i = pl.program_id(0)
    members, layers, nx, ny = u_ref.shape
    lane = lax.broadcasted_iota(jnp.int32, (nx, ny), 1)
    first_lane, last_lane = lane == 0, lane == ny - 1
    half = step_size * 0.5

    @pl.when(i == 0)
    def _():
        set_lanes(pos_ref[...], lanes, range(layers), nx, ny)

    def member(b, _):
        u = u_ref[b, 0].astype(F32)
        k = k_ref[b, 0].astype(F32)
        below = None
        for z in range(layers):
            ku = k * u
            un = jnp.where(last_lane, 0.0, pltpu.roll(u, ny - 1, 1))
            kn = jnp.where(last_lane, 0.0, pltpu.roll(k, ny - 1, 1))
            f = (k + kn) * (un - u)
            acc = f - jnp.where(first_lane, ku, pltpu.roll(f, 1, 1))
            f = (k + shift_up(k)) * (shift_up(u) - u)
            acc = acc + (f - shift_down(f, ku[:1]))
            if below is not None:
                acc = acc - below
            u_now = u
            if z < layers - 1:
                u_next = u_ref[b, z + 1].astype(F32)
                k_next = k_ref[b, z + 1].astype(F32)
                below = (k + k_next) * (u_next - u)
                acc = acc + below
                u, k = u_next, k_next
            value = u_now + half * acc
            out_ref[b, z] = value
            put(pair, pl.ds(pl.multiple_of(b * nx, nx), nx), z, value)
        return 0

    lax.fori_loop(0, members, member, 0)
    pick(pair, lanes, pos_ref[...] // ny % nx, sums, i * members * 8, nx)

    @pl.when(i == pl.num_programs(0) - 1)
    def _():
        picked_ref[...] = add_eights(sums[...])


def stencil(pos, u, k):
    m, layers, nx, ny = u.shape
    per = GROUP
    block = pl.BlockSpec((per, layers, nx, ny), lambda i: (i, 0, 0, 0))
    slots = pos.shape[1]
    return pl.pallas_call(
        stencil_kernel,
        grid=(m // per,),
        in_specs=[pl.BlockSpec(pos.shape, lambda i: (0, 0)), block, block],
        out_specs=[block, pl.BlockSpec((m, slots), lambda i: (0, 0))],
        out_shape=[
            jax.ShapeDtypeStruct(u.shape, F32),
            jax.ShapeDtypeStruct((m, slots), F32),
        ],
        scratch_shapes=[
            pltpu.VMEM((2 * layers * ny, slots), jnp.bfloat16),
            pltpu.VMEM((per * nx, 2 * layers * ny), jnp.bfloat16),
            pltpu.VMEM((8 * m, slots), F32),
        ],
        compiler_params=pltpu.CompilerParams(vmem_limit_bytes=24 << 20),
        cost_estimate=pl.CostEstimate(
            flops=40 * u.size, bytes_accessed=8 * u.size, transcendentals=0
        ),
    )(pos, u, k)


def face_flux(own, halo, b):
    u, k = own[0, b].astype(F32), own[1, b].astype(F32)
    return (step_size * 0.5) * ((k + halo[1, b].astype(F32)) * (halo[0, b].astype(F32) - u))


def readings_kernel(
    last_layer, pos_ref, head_ref, last_ref, lo_ref, hi_ref, partial_ref, params_ref, out_ref,
    lanes, pair, sums
):
    _, members, nx, ny = head_ref.shape
    slots, per = partial_ref.shape[1], pair.shape[0] // nx
    set_lanes(pos_ref[...], lanes, (0, last_layer), nx, ny)
    x = pos_ref[...] // ny % nx

    def group(q, _):
        def member(b, _):
            rows = pl.ds(pl.multiple_of(b * nx, nx), nx)
            put(pair, rows, 0, face_flux(head_ref, lo_ref, q * per + b))
            put(pair, rows, 1, face_flux(last_ref, hi_ref, q * per + b))
            return 0

        lax.fori_loop(0, per, member, 0, unroll=4)
        pick(pair, lanes, x, sums, q * per * 8, nx)
        return 0

    lax.fori_loop(0, members // per, group, 0)
    out_ref[:, :slots] = partial_ref[...] + add_eights(sums[...])
    out_ref[:, slots:] = params_ref[...]


def readings(pos, head, last, lo, hi, partial, params, layers):
    _, m, nx, ny = head.shape
    slots = pos.shape[1]
    vmem = pl.BlockSpec(memory_space=pltpu.VMEM)
    return pl.pallas_call(
        lambda *refs: readings_kernel(layers - 1, *refs),
        in_specs=[vmem] * 7,
        out_specs=vmem,
        out_shape=jax.ShapeDtypeStruct((m, slots + params.shape[1]), F32),
        scratch_shapes=[
            pltpu.VMEM((4 * ny, slots), jnp.bfloat16),
            pltpu.VMEM((2 * GROUP * nx, 4 * ny), jnp.bfloat16),
            pltpu.VMEM((8 * m, slots), F32),
        ],
        compiler_params=pltpu.CompilerParams(vmem_limit_bytes=10 << 20),
        cost_estimate=pl.CostEstimate(
            flops=8 * m * nx * ny, bytes_accessed=8 << 20, transcendentals=0
        ),
    )(pos, head, last, lo, hi, partial, params)


def face_kernel(u_ref, k_ref, halo_ref, in_ref, out_ref):
    def member(b, _):
        u, k = u_ref[b, 0].astype(F32), k_ref[b, 0].astype(F32)
        flux = (k + halo_ref[1, b].astype(F32)) * (halo_ref[0, b].astype(F32) - u)
        out_ref[b, 0] = in_ref[b, 0] + (step_size * 0.5) * flux
        return 0

    lax.fori_loop(0, in_ref.shape[0], member, 0)


def add_face(u, k, halo, states, layer):
    m, _, nx, ny = states.shape
    per = 16
    face = pl.BlockSpec((per, 1, nx, ny), lambda g: (g, layer, 0, 0))
    return pl.pallas_call(
        face_kernel,
        grid=(m // per,),
        in_specs=[face, face, pl.BlockSpec((2, per, nx, ny), lambda g: (0, g, 0, 0)), face],
        out_specs=face,
        out_shape=jax.ShapeDtypeStruct(states.shape, F32),
        input_output_aliases={3: 0},
        compiler_params=pltpu.CompilerParams(vmem_limit_bytes=58 << 20),
        cost_estimate=pl.CostEstimate(
            flops=4 * m * nx * ny, bytes_accessed=16 * m * nx * ny, transcendentals=0
        ),
    )(u, k, halo, states)


def contract(a, b, dims):
    return lax.dot_general(a, b, (dims, ((), ())), precision=HIGH, preferred_element_type=F32)


def gram_kernel(scale, count_ref, core_ref, *refs):
    blocks, (noise, values, std, sum_ref, anomaly_ref) = refs[:8], refs[8:]
    rows = blocks[0].shape[0]
    n = 4 * rows
    slots = noise.shape[1]
    readings = [b[:, :slots] for b in blocks]
    own = readings[0]
    total = own
    for b in readings[1:]:
        total = total + b
    centre = jnp.sum(total, axis=0, keepdims=True) * (1.0 / (8 * rows))
    live = lax.broadcasted_iota(jnp.int32, centre.shape, 1) < count_ref[0]
    weight = jnp.where(live, 1.0 / (std[...] * scale), 0.0)
    first = jnp.concatenate([(b - centre) * weight for b in readings[:4]], axis=0)
    second = jnp.concatenate([(b - centre) * weight for b in readings[4:]], axis=0)
    misfit = jnp.where(live, (values[...] - own) / std[...] + noise[...], 0.0)
    on_first = contract(
        jnp.concatenate([first, second[: n // 2], misfit], axis=0), first, ((1,), (1,))
    )
    on_second = contract(
        jnp.concatenate([first[n // 2 :], misfit], axis=0), second, ((1,), (1,))
    )
    params = jnp.concatenate([b[:, slots:] for b in blocks], axis=0)
    mean = jnp.sum(params, axis=0, keepdims=True) * (1.0 / (2 * n))
    anomaly_ref[...] = (params - mean) * (1.0 / scale)
    is_first = core_ref[0] == 0
    half = n // 2
    left = lax.broadcasted_iota(jnp.int32, (half, n), 1) < half
    sum_ref[:half] = jnp.where(left, on_first[:half], on_first[half:n])
    turned = pltpu.roll(on_first[:half], half, 1)
    sum_ref[half : half + half // 2] = jnp.where(
        left[: half // 2], turned[: half // 2], on_first[half // 2 : half]
    )
    at = half + half // 2
    sum_ref[at : at + half] = jnp.where(is_first, on_first[n : n + half], on_second[:half])
    sum_ref[at + half : at + half + rows] = on_first[n + half :]
    sum_ref[at + half + rows :] = on_second[half:]


def gram(count, core, blocks, noise, values, std, ens_scale):
    rows = blocks[0].shape[0]
    vmem = pl.BlockSpec(memory_space=pltpu.VMEM)
    return pl.pallas_call(
        lambda *refs: gram_kernel(ens_scale, *refs),
        in_specs=[pl.BlockSpec(memory_space=pltpu.SMEM)] * 2 + [vmem] * 11,
        out_specs=[vmem, vmem],
        out_shape=[
            jax.ShapeDtypeStruct((7 * rows, 4 * rows), F32),
            jax.ShapeDtypeStruct((8 * rows, blocks[0].shape[1] - noise.shape[1]), F32),
        ],
        compiler_params=pltpu.CompilerParams(vmem_limit_bytes=16 << 20),
    )(count, core, *blocks, noise, values.reshape(1, -1), std.reshape(1, -1))


def inverse4(k):
    r = 1.0 / (k[0][0] * k[1][1] - k[0][1] * k[0][1])
    a00, a01, a11 = k[1][1] * r, -k[0][1] * r, k[0][0] * r
    t00, t01 = a00 * k[0][2] + a01 * k[1][2], a00 * k[0][3] + a01 * k[1][3]
    t10, t11 = a01 * k[0][2] + a11 * k[1][2], a01 * k[0][3] + a11 * k[1][3]
    s00 = k[2][2] - (k[0][2] * t00 + k[1][2] * t10)
    s01 = k[2][3] - (k[0][2] * t01 + k[1][2] * t11)
    s11 = k[3][3] - (k[0][3] * t01 + k[1][3] * t11)
    q = 1.0 / (s00 * s11 - s01 * s01)
    i00, i01, i11 = s11 * q, -s01 * q, s00 * q
    v00, v01 = t00 * i00 + t01 * i01, t00 * i01 + t01 * i11
    v10, v11 = t10 * i00 + t11 * i01, t10 * i01 + t11 * i11
    b00 = a00 + v00 * t00 + v01 * t01
    b01 = a01 + v00 * t10 + v01 * t11
    b11 = a11 + v10 * t10 + v11 * t11
    return [
        [b00, b01, -v00, -v01],
        [b01, b11, -v10, -v11],
        [-v00, -v10, i00, i01],
        [-v01, -v11, i01, i11],
    ]


def pivoted_inverse(p):
    n = p.shape[0]
    tiles = [p[t : t + 8] for t in range(0, n, 8)]
    row = lax.broadcasted_iota(jnp.int32, (8, n), 0)
    lane = lax.broadcasted_iota(jnp.int32, (8, n), 1)
    lane1 = lax.broadcasted_iota(jnp.int32, (1, n), 1)

    def spread(tile, at):
        return jnp.broadcast_to(tile[:, at : at + 1], (8, n))

    def entries(tile, at):
        columns = [spread(tile, at + b) for b in range(4)]
        return [[columns[b][at % 8 + a : at % 8 + a + 1] for b in range(4)] for a in range(4)]

    def dot4(x, y):
        return (x[0] * y[0] + x[1] * y[1]) + (x[2] * y[2] + x[3] * y[3])

    inv = inverse4(entries(tiles[0], 0))
    for i in range(0, n, 4):
        here, off = i // 8, i % 8
        cols = [[spread(t, i + b) for t in tiles] for b in range(4)]
        ahead = None
        if i + 4 < n:
            there, shift = (i + 4) // 8, (i + 4) % 8
            q = entries(tiles[there], i + 4)
            c = [[cols[m][there][shift + a : shift + a + 1] for m in range(4)] for a in range(4)]
            w = [[dot4(inv[m], c[b]) for m in range(4)] for b in range(4)]
            ahead = inverse4(
                [[q[a][b] - dot4(c[a], w[b]) if a <= b else None for b in range(4)] for a in range(4)]
            )
        inside1 = (lane1 >= i) & (lane1 < i + 4)
        e = [
            jnp.where(
                inside1, jnp.where(lane1 == i + a, 1.0, 0.0), tiles[here][off + a : off + a + 1]
            )
            for a in range(4)
        ]
        new = [dot4(inv[a], e) for a in range(4)]
        inside = (lane >= i) & (lane < i + 4)
        for t in range(n // 8):
            rest = jnp.where(inside, 0.0, tiles[t])
            tiles[t] = rest - (
                (cols[0][t] * new[0] + cols[1][t] * new[1])
                + (cols[2][t] * new[2] + cols[3][t] * new[3])
            )
        for a in range(4):
            tiles[here] = jnp.where(row == off + a, new[a], tiles[here])
        inv = ahead
    return jnp.concatenate(tiles, axis=0)


def spd_inverse(corner, side, rest):
    first = pivoted_inverse(corner)
    ahead = contract(first, side, ((1,), (0,)))
    second = pivoted_inverse(rest - contract(side, ahead, ((0,), (0,))))
    mixed = contract(ahead, second, ((1,), (0,)))
    top = jnp.concatenate([first + contract(mixed, ahead, ((1,), (1,))), -mixed], axis=1)
    return jnp.concatenate([top, jnp.concatenate([-mixed.T, second], axis=1)], axis=0)


def square(sum_ref):
    h = sum_ref.shape[1] // 2
    pair, side = sum_ref[:h], sum_ref[h : h + h // 2]
    eye = identity(h)
    return (
        pair[:, :h] + eye,
        jnp.concatenate([side[:, :h], side[:, h:]], axis=0),
        pair[:, h:] + eye,
    )


def identity(n):
    return jnp.where(
        lax.broadcasted_iota(jnp.int32, (n, n), 0) == lax.broadcasted_iota(jnp.int32, (n, n), 1),
        1.0,
        0.0,
    )


def inverse_kernel(sum_ref, out_ref):
    out_ref[...] = spd_inverse(*square(sum_ref))


def inverse(sums):
    n = sums.shape[1]
    vmem = pl.BlockSpec(memory_space=pltpu.VMEM)
    return pl.pallas_call(
        inverse_kernel,
        in_specs=[vmem],
        out_specs=vmem,
        out_shape=jax.ShapeDtypeStruct((n, n), F32),
        compiler_params=pltpu.CompilerParams(vmem_limit_bytes=4 << 20),
        cost_estimate=pl.CostEstimate(flops=4 << 30, bytes_accessed=1 << 20, transcendentals=0),
    )(sums)


def update_kernel(core_ref, inv_ref, sum_ref, other_ref, anomaly_ref, params_ref, out_ref):
    n = inv_ref.shape[0]
    half, rows = n // 2, params_ref.shape[0]
    anomaly = anomaly_ref[...]
    is_first = core_ref[0] == 0
    at = half + half // 2
    mine, theirs = sum_ref[at : at + half], other_ref[at : at + half]
    product = jnp.concatenate(
        [jnp.where(is_first, mine, theirs), jnp.where(is_first, theirs, mine)], axis=0
    )
    fs = jnp.where(is_first, product.T, product)
    right = contract(inv_ref[...], jnp.concatenate([fs, anomaly[:n]], axis=1), ((1,), (0,)))
    down = contract(fs, right, ((0,), (0,)))
    corner, side, rest = square(other_ref)
    second = spd_inverse(
        corner - down[:half, :half], side - down[:half, half:n], rest - down[half:, half:n]
    )
    x_second = contract(second, anomaly[n:] - down[:, n:], ((1,), (0,)))
    x_first = right[:, n:] - contract(right[:, :n], x_second, ((1,), (0,)))
    at = at + half
    cross_first, cross_second = sum_ref[at : at + rows], sum_ref[at + rows :]
    out_ref[...] = params_ref[...] + (
        contract(cross_first, x_first, ((1,), (0,))) + contract(cross_second, x_second, ((1,), (0,)))
    )


def update(core, inv, sums, other, anomaly, params):
    vmem = pl.BlockSpec(memory_space=pltpu.VMEM)
    return pl.pallas_call(
        update_kernel,
        in_specs=[pl.BlockSpec(memory_space=pltpu.SMEM)] + [vmem] * 5,
        out_specs=vmem,
        out_shape=jax.ShapeDtypeStruct(params.shape, F32),
        compiler_params=pltpu.CompilerParams(vmem_limit_bytes=8 << 20),
    )(core, inv, sums, other, anomaly, params)


def around_x(a):
    return [a] + [
        lax.ppermute(
            a, "space", [(z * 4 + x, z * 4 + (x + s) % 4) for z in range(4) for x in range(4)]
        )
        for s in (1, 3, 2)
    ]


def around_z(a):
    return [a] + [
        lax.ppermute(
            a, "space", [(z * 4 + x, (z + s) % 4 * 4 + x) for z in range(4) for x in range(4)]
        )
        for s in (1, 3, 2)
    ]


def around_y(a):
    return [a] + [
        lax.ppermute(a, "ens", [(e, (e + 2 * s) % 8) for e in range(8)]) for s in (1, 3, 2)
    ]


def partner(a):
    return lax.ppermute(a, "ens", [(e, e ^ 1) for e in range(8)])


def total4(parts):
    return (parts[0] + parts[1]) + (parts[2] + parts[3])


def shards(u, k, pos, count, values, std, noise, params):
    spaces = lax.axis_size("space")
    ens_scale = math.sqrt(u.shape[0] * lax.axis_size("ens") - 1.0)
    last = jnp.stack([u[:, -1], k[:, -1]])
    head = jnp.stack([u[:, 0], k[:, 0]])
    lo = lax.ppermute(last, "space", [(i, i + 1) for i in range(spaces - 1)])
    hi = lax.ppermute(head, "space", [(i + 1, i) for i in range(spaces - 1)])
    cells = pos.reshape(1, -1)
    states, partial = stencil(cells, u, k)
    picked = readings(cells, head, last, lo, hi, partial, params, u.shape[1])
    mine = around_y(picked)
    blocks = mine + [partner(a) for a in mine]

    core = (lax.axis_index("ens") % 2).astype(jnp.int32).reshape(1)
    sums, anomaly = gram(count, core, blocks, noise, values, std, ens_scale)
    lo, sums = lax.optimization_barrier((lo, sums))
    states = add_face(u, k, lo, states, 0)
    sums, states, hi = lax.optimization_barrier((total4(around_x(sums)), states, hi))
    parts = around_z(sums)
    states = add_face(u, k, hi, states, u.shape[1] - 1)
    sums, states = lax.optimization_barrier((total4(parts), states))
    other = partner(sums)
    inv = inverse(sums)
    return update(core, inv, sums, other, anomaly, params), states


def solution(mesh):
    in_specs = (
        P("ens", "space", None, None),
        P("ens", "space", None, None),
        P("space"),
        P("space"),
        P("space"),
        P("space"),
        P("ens", "space"),
        P("ens", "space"),
    )
    out_specs = (P("ens", "space"), P("ens", "space", None, None))
    return jax.shard_map(shards, mesh=mesh, in_specs=in_specs, out_specs=out_specs, check_vma=False)
```

```python
import math

import jax
import jax.numpy as jnp
from jax import lax
from jax.experimental import pallas as pl
from jax.experimental.pallas import tpu as pltpu
from jax.sharding import PartitionSpec as P

step_size = 0.08
HIGH = lax.Precision.HIGHEST
F32 = jnp.float32


def shift_down(a, first):
    return jnp.concatenate([first, a[:-1]], axis=0)


def shift_up(a):
    return jnp.concatenate([a[1:], jnp.zeros_like(a[:1])], axis=0)


GROUP = 8


def set_lanes(pos, lanes, layers, nx, ny):
    slots = lanes.shape[1]
    lane = lax.broadcasted_iota(jnp.int32, (ny, slots), 0)
    for section, layer in enumerate(layers):
        own = jnp.where(pos // (nx * ny) == layer, pos % ny, -1)
        hot = jnp.where(lane == own, 1.0, 0.0).astype(jnp.bfloat16)
        base = 2 * section * ny
        lanes[base : base + ny] = hot
        lanes[base + ny : base + 2 * ny] = hot


def put(pair, rows, section, value):
    ny = value.shape[1]
    high = value.astype(jnp.bfloat16)
    base = 2 * section * ny
    pair[rows, base : base + ny] = high
    pair[rows, base + ny : base + 2 * ny] = (value - high.astype(F32)).astype(jnp.bfloat16)


def pick(pair, lanes, x, sums, base, nx, chunk=256):
    slots = lanes.shape[1]
    row = lax.broadcasted_iota(jnp.int32, (nx, chunk), 0)
    for c in range(0, slots, chunk):
        t = jnp.dot(pair[...], lanes[:, c : c + chunk], preferred_element_type=F32)
        hit = row == x[:, c : c + chunk]
        for b in range(pair.shape[0] // nx):
            part = jnp.where(hit, t[b * nx : (b + 1) * nx], 0.0)
            at = pl.ds(pl.multiple_of(base + b * 8, 8), 8)
            sums[at, c : c + chunk] = jnp.sum(part.reshape(nx // 8, 8, chunk), axis=0)


def add_eights(sums):
    m = sums.shape[0] // 8
    member = lax.broadcasted_iota(jnp.int32, (m, 8 * m), 1) // 8
    add = jnp.where(member == lax.broadcasted_iota(jnp.int32, (m, 8 * m), 0), 1.0, 0.0)
    return contract(add, sums, ((1,), (0,)))


def stencil_kernel(pos_ref, u_ref, k_ref, out_ref, picked_ref, lanes, pair, sums):
    i = pl.program_id(0)
    members, layers, nx, ny = u_ref.shape
    lane = lax.broadcasted_iota(jnp.int32, (nx, ny), 1)
    first_lane, last_lane = lane == 0, lane == ny - 1
    half = step_size * 0.5

    @pl.when(i == 0)
    def _():
        set_lanes(pos_ref[...], lanes, range(layers), nx, ny)

    def member(b, _):
        u = u_ref[b, 0].astype(F32)
        k = k_ref[b, 0].astype(F32)
        below = None
        for z in range(layers):
            ku = k * u
            un = jnp.where(last_lane, 0.0, pltpu.roll(u, ny - 1, 1))
            kn = jnp.where(last_lane, 0.0, pltpu.roll(k, ny - 1, 1))
            f = (k + kn) * (un - u)
            acc = f - jnp.where(first_lane, ku, pltpu.roll(f, 1, 1))
            f = (k + shift_up(k)) * (shift_up(u) - u)
            acc = acc + (f - shift_down(f, ku[:1]))
            if below is not None:
                acc = acc - below
            u_now = u
            if z < layers - 1:
                u_next = u_ref[b, z + 1].astype(F32)
                k_next = k_ref[b, z + 1].astype(F32)
                below = (k + k_next) * (u_next - u)
                acc = acc + below
                u, k = u_next, k_next
            value = u_now + half * acc
            out_ref[b, z] = value
            put(pair, pl.ds(pl.multiple_of(b * nx, nx), nx), z, value)
        return 0

    lax.fori_loop(0, members, member, 0)
    pick(pair, lanes, pos_ref[...] // ny % nx, sums, i * members * 8, nx)

    @pl.when(i == pl.num_programs(0) - 1)
    def _():
        picked_ref[...] = add_eights(sums[...])


def stencil(pos, u, k):
    m, layers, nx, ny = u.shape
    per = GROUP
    block = pl.BlockSpec((per, layers, nx, ny), lambda i: (i, 0, 0, 0))
    slots = pos.shape[1]
    return pl.pallas_call(
        stencil_kernel,
        grid=(m // per,),
        in_specs=[pl.BlockSpec(pos.shape, lambda i: (0, 0)), block, block],
        out_specs=[block, pl.BlockSpec((m, slots), lambda i: (0, 0))],
        out_shape=[
            jax.ShapeDtypeStruct(u.shape, F32),
            jax.ShapeDtypeStruct((m, slots), F32),
        ],
        scratch_shapes=[
            pltpu.VMEM((2 * layers * ny, slots), jnp.bfloat16),
            pltpu.VMEM((per * nx, 2 * layers * ny), jnp.bfloat16),
            pltpu.VMEM((8 * m, slots), F32),
        ],
        compiler_params=pltpu.CompilerParams(vmem_limit_bytes=24 << 20),
        cost_estimate=pl.CostEstimate(
            flops=40 * u.size, bytes_accessed=8 * u.size, transcendentals=0
        ),
    )(pos, u, k)


def face_flux(own, halo, b):
    u, k = own[0, b].astype(F32), own[1, b].astype(F32)
    return (step_size * 0.5) * ((k + halo[1, b].astype(F32)) * (halo[0, b].astype(F32) - u))


def readings_kernel(
    last_layer, pos_ref, head_ref, last_ref, lo_ref, hi_ref, partial_ref, params_ref, out_ref,
    lanes, pair, sums
):
    _, members, nx, ny = head_ref.shape
    slots, per = partial_ref.shape[1], pair.shape[0] // nx
    set_lanes(pos_ref[...], lanes, (0, last_layer), nx, ny)
    x = pos_ref[...] // ny % nx

    def group(q, _):
        def member(b, _):
            rows = pl.ds(pl.multiple_of(b * nx, nx), nx)
            put(pair, rows, 0, face_flux(head_ref, lo_ref, q * per + b))
            put(pair, rows, 1, face_flux(last_ref, hi_ref, q * per + b))
            return 0

        lax.fori_loop(0, per, member, 0, unroll=4)
        pick(pair, lanes, x, sums, q * per * 8, nx)
        return 0

    lax.fori_loop(0, members // per, group, 0)
    out_ref[:, :slots] = partial_ref[...] + add_eights(sums[...])
    out_ref[:, slots:] = params_ref[...]


def readings(pos, head, last, lo, hi, partial, params, layers):
    _, m, nx, ny = head.shape
    slots = pos.shape[1]
    vmem = pl.BlockSpec(memory_space=pltpu.VMEM)
    return pl.pallas_call(
        lambda *refs: readings_kernel(layers - 1, *refs),
        in_specs=[vmem] * 7,
        out_specs=vmem,
        out_shape=jax.ShapeDtypeStruct((m, slots + params.shape[1]), F32),
        scratch_shapes=[
            pltpu.VMEM((4 * ny, slots), jnp.bfloat16),
            pltpu.VMEM((2 * GROUP * nx, 4 * ny), jnp.bfloat16),
            pltpu.VMEM((8 * m, slots), F32),
        ],
        compiler_params=pltpu.CompilerParams(vmem_limit_bytes=10 << 20),
        cost_estimate=pl.CostEstimate(
            flops=8 * m * nx * ny, bytes_accessed=8 << 20, transcendentals=0
        ),
    )(pos, head, last, lo, hi, partial, params)


def face_kernel(u_ref, k_ref, halo_ref, in_ref, out_ref):
    def member(b, _):
        u, k = u_ref[b, 0].astype(F32), k_ref[b, 0].astype(F32)
        flux = (k + halo_ref[1, b].astype(F32)) * (halo_ref[0, b].astype(F32) - u)
        out_ref[b, 0] = in_ref[b, 0] + (step_size * 0.5) * flux
        return 0

    lax.fori_loop(0, in_ref.shape[0], member, 0)


def add_face(u, k, halo, states, layer):
    m, _, nx, ny = states.shape
    per = 16
    face = pl.BlockSpec((per, 1, nx, ny), lambda g: (g, layer, 0, 0))
    return pl.pallas_call(
        face_kernel,
        grid=(m // per,),
        in_specs=[face, face, pl.BlockSpec((2, per, nx, ny), lambda g: (0, g, 0, 0)), face],
        out_specs=face,
        out_shape=jax.ShapeDtypeStruct(states.shape, F32),
        input_output_aliases={3: 0},
        compiler_params=pltpu.CompilerParams(vmem_limit_bytes=58 << 20),
        cost_estimate=pl.CostEstimate(
            flops=4 * m * nx * ny, bytes_accessed=16 * m * nx * ny, transcendentals=0
        ),
    )(u, k, halo, states)


def contract(a, b, dims):
    return lax.dot_general(a, b, (dims, ((), ())), precision=HIGH, preferred_element_type=F32)


def gram_kernel(scale, count_ref, core_ref, *refs):
    blocks, (noise, values, std, sum_ref, anomaly_ref) = refs[:8], refs[8:]
    rows = blocks[0].shape[0]
    n = 4 * rows
    slots = noise.shape[1]
    readings = [b[:, :slots] for b in blocks]
    own = readings[0]
    total = own
    for b in readings[1:]:
        total = total + b
    centre = jnp.sum(total, axis=0, keepdims=True) * (1.0 / (8 * rows))
    live = lax.broadcasted_iota(jnp.int32, centre.shape, 1) < count_ref[0]
    weight = jnp.where(live, 1.0 / (std[...] * scale), 0.0)
    first = jnp.concatenate([(b - centre) * weight for b in readings[:4]], axis=0)
    second = jnp.concatenate([(b - centre) * weight for b in readings[4:]], axis=0)
    misfit = jnp.where(live, (values[...] - own) / std[...] + noise[...], 0.0)
    on_first = contract(
        jnp.concatenate([first, second[: n // 2], misfit], axis=0), first, ((1,), (1,))
    )
    on_second = contract(
        jnp.concatenate([first[n // 2 :], misfit], axis=0), second, ((1,), (1,))
    )
    params = jnp.concatenate([b[:, slots:] for b in blocks], axis=0)
    mean = jnp.sum(params, axis=0, keepdims=True) * (1.0 / (2 * n))
    anomaly_ref[...] = (params - mean) * (1.0 / scale)
    is_first = core_ref[0] == 0
    half = n // 2
    left = lax.broadcasted_iota(jnp.int32, (half, n), 1) < half
    sum_ref[:half] = jnp.where(left, on_first[:half], on_first[half:n])
    turned = pltpu.roll(on_first[:half], half, 1)
    sum_ref[half : half + half // 2] = jnp.where(
        left[: half // 2], turned[: half // 2], on_first[half // 2 : half]
    )
    at = half + half // 2
    sum_ref[at : at + half] = jnp.where(is_first, on_first[n : n + half], on_second[:half])
    sum_ref[at + half : at + half + rows] = on_first[n + half :]
    sum_ref[at + half + rows :] = on_second[half:]


def gram(count, core, blocks, noise, values, std, ens_scale):
    rows = blocks[0].shape[0]
    vmem = pl.BlockSpec(memory_space=pltpu.VMEM)
    return pl.pallas_call(
        lambda *refs: gram_kernel(ens_scale, *refs),
        in_specs=[pl.BlockSpec(memory_space=pltpu.SMEM)] * 2 + [vmem] * 11,
        out_specs=[vmem, vmem],
        out_shape=[
            jax.ShapeDtypeStruct((7 * rows, 4 * rows), F32),
            jax.ShapeDtypeStruct((8 * rows, blocks[0].shape[1] - noise.shape[1]), F32),
        ],
        compiler_params=pltpu.CompilerParams(vmem_limit_bytes=16 << 20),
    )(count, core, *blocks, noise, values.reshape(1, -1), std.reshape(1, -1))


def inverse4(k):
    r = 1.0 / (k[0][0] * k[1][1] - k[0][1] * k[0][1])
    a00, a01, a11 = k[1][1] * r, -k[0][1] * r, k[0][0] * r
    t00, t01 = a00 * k[0][2] + a01 * k[1][2], a00 * k[0][3] + a01 * k[1][3]
    t10, t11 = a01 * k[0][2] + a11 * k[1][2], a01 * k[0][3] + a11 * k[1][3]
    s00 = k[2][2] - (k[0][2] * t00 + k[1][2] * t10)
    s01 = k[2][3] - (k[0][2] * t01 + k[1][2] * t11)
    s11 = k[3][3] - (k[0][3] * t01 + k[1][3] * t11)
    q = 1.0 / (s00 * s11 - s01 * s01)
    i00, i01, i11 = s11 * q, -s01 * q, s00 * q
    v00, v01 = t00 * i00 + t01 * i01, t00 * i01 + t01 * i11
    v10, v11 = t10 * i00 + t11 * i01, t10 * i01 + t11 * i11
    b00 = a00 + v00 * t00 + v01 * t01
    b01 = a01 + v00 * t10 + v01 * t11
    b11 = a11 + v10 * t10 + v11 * t11
    return [
        [b00, b01, -v00, -v01],
        [b01, b11, -v10, -v11],
        [-v00, -v10, i00, i01],
        [-v01, -v11, i01, i11],
    ]


def pivoted_inverse(p):
    n = p.shape[0]
    tiles = [p[t : t + 8] for t in range(0, n, 8)]
    row = lax.broadcasted_iota(jnp.int32, (8, n), 0)
    lane = lax.broadcasted_iota(jnp.int32, (8, n), 1)
    lane1 = lax.broadcasted_iota(jnp.int32, (1, n), 1)

    def spread(tile, at):
        return jnp.broadcast_to(tile[:, at : at + 1], (8, n))

    def entries(tile, at):
        columns = [spread(tile, at + b) for b in range(4)]
        return [[columns[b][at % 8 + a : at % 8 + a + 1] for b in range(4)] for a in range(4)]

    def dot4(x, y):
        return (x[0] * y[0] + x[1] * y[1]) + (x[2] * y[2] + x[3] * y[3])

    inv = inverse4(entries(tiles[0], 0))
    for i in range(0, n, 4):
        here, off = i // 8, i % 8
        cols = [[spread(t, i + b) for t in tiles] for b in range(4)]
        ahead = None
        if i + 4 < n:
            there, shift = (i + 4) // 8, (i + 4) % 8
            q = entries(tiles[there], i + 4)
            c = [[cols[m][there][shift + a : shift + a + 1] for m in range(4)] for a in range(4)]
            w = [[dot4(inv[m], c[b]) for m in range(4)] for b in range(4)]
            ahead = inverse4(
                [[q[a][b] - dot4(c[a], w[b]) if a <= b else None for b in range(4)] for a in range(4)]
            )
        inside1 = (lane1 >= i) & (lane1 < i + 4)
        e = [
            jnp.where(
                inside1, jnp.where(lane1 == i + a, 1.0, 0.0), tiles[here][off + a : off + a + 1]
            )
            for a in range(4)
        ]
        new = [dot4(inv[a], e) for a in range(4)]
        inside = (lane >= i) & (lane < i + 4)
        for t in range(n // 8):
            rest = jnp.where(inside, 0.0, tiles[t])
            tiles[t] = rest - (
                (cols[0][t] * new[0] + cols[1][t] * new[1])
                + (cols[2][t] * new[2] + cols[3][t] * new[3])
            )
        for a in range(4):
            tiles[here] = jnp.where(row == off + a, new[a], tiles[here])
        inv = ahead
    return jnp.concatenate(tiles, axis=0)


def spd_inverse(corner, side, rest):
    first = pivoted_inverse(corner)
    ahead = contract(first, side, ((1,), (0,)))
    second = pivoted_inverse(rest - contract(side, ahead, ((0,), (0,))))
    mixed = contract(ahead, second, ((1,), (0,)))
    top = jnp.concatenate([first + contract(mixed, ahead, ((1,), (1,))), -mixed], axis=1)
    return jnp.concatenate([top, jnp.concatenate([-mixed.T, second], axis=1)], axis=0)


def square(sum_ref):
    h = sum_ref.shape[1] // 2
    pair, side = sum_ref[:h], sum_ref[h : h + h // 2]
    eye = identity(h)
    return (
        pair[:, :h] + eye,
        jnp.concatenate([side[:, :h], side[:, h:]], axis=0),
        pair[:, h:] + eye,
    )


def identity(n):
    return jnp.where(
        lax.broadcasted_iota(jnp.int32, (n, n), 0) == lax.broadcasted_iota(jnp.int32, (n, n), 1),
        1.0,
        0.0,
    )


def inverse_kernel(sum_ref, out_ref):
    out_ref[...] = spd_inverse(*square(sum_ref))


def inverse(sums):
    n = sums.shape[1]
    vmem = pl.BlockSpec(memory_space=pltpu.VMEM)
    return pl.pallas_call(
        inverse_kernel,
        in_specs=[vmem],
        out_specs=vmem,
        out_shape=jax.ShapeDtypeStruct((n, n), F32),
        compiler_params=pltpu.CompilerParams(vmem_limit_bytes=4 << 20),
        cost_estimate=pl.CostEstimate(flops=4 << 30, bytes_accessed=1 << 20, transcendentals=0),
    )(sums)


def update_kernel(core_ref, inv_ref, sum_ref, other_ref, anomaly_ref, params_ref, out_ref):
    n = inv_ref.shape[0]
    half, rows = n // 2, params_ref.shape[0]
    anomaly = anomaly_ref[...]
    is_first = core_ref[0] == 0
    at = half + half // 2
    mine, theirs = sum_ref[at : at + half], other_ref[at : at + half]
    product = jnp.concatenate(
        [jnp.where(is_first, mine, theirs), jnp.where(is_first, theirs, mine)], axis=0
    )
    fs = jnp.where(is_first, product.T, product)
    right = contract(inv_ref[...], jnp.concatenate([fs, anomaly[:n]], axis=1), ((1,), (0,)))
    down = contract(fs, right, ((0,), (0,)))
    corner, side, rest = square(other_ref)
    second = spd_inverse(
        corner - down[:half, :half], side - down[:half, half:n], rest - down[half:, half:n]
    )
    x_second = contract(second, anomaly[n:] - down[:, n:], ((1,), (0,)))
    x_first = right[:, n:] - contract(right[:, :n], x_second, ((1,), (0,)))
    at = at + half
    cross_first, cross_second = sum_ref[at : at + rows], sum_ref[at + rows :]
    out_ref[...] = params_ref[...] + (
        contract(cross_first, x_first, ((1,), (0,))) + contract(cross_second, x_second, ((1,), (0,)))
    )


def update(core, inv, sums, other, anomaly, params):
    vmem = pl.BlockSpec(memory_space=pltpu.VMEM)
    return pl.pallas_call(
        update_kernel,
        in_specs=[pl.BlockSpec(memory_space=pltpu.SMEM)] + [vmem] * 5,
        out_specs=vmem,
        out_shape=jax.ShapeDtypeStruct(params.shape, F32),
        compiler_params=pltpu.CompilerParams(vmem_limit_bytes=8 << 20),
    )(core, inv, sums, other, anomaly, params)


def around_x(a):
    return [a] + [
        lax.ppermute(
            a, "space", [(z * 4 + x, z * 4 + (x + s) % 4) for z in range(4) for x in range(4)]
        )
        for s in (1, 3, 2)
    ]


def around_z(a):
    return [a] + [
        lax.ppermute(
            a, "space", [(z * 4 + x, (z + s) % 4 * 4 + x) for z in range(4) for x in range(4)]
        )
        for s in (1, 3, 2)
    ]


def around_y(a):
    return [a] + [
        lax.ppermute(a, "ens", [(e, (e + 2 * s) % 8) for e in range(8)]) for s in (1, 3, 2)
    ]


def partner(a):
    return lax.ppermute(a, "ens", [(e, e ^ 1) for e in range(8)])


def total4(parts):
    return (parts[0] + parts[1]) + (parts[2] + parts[3])


def shards(u, k, pos, count, values, std, noise, params):
    spaces = lax.axis_size("space")
    ens_scale = math.sqrt(u.shape[0] * lax.axis_size("ens") - 1.0)
    last = jnp.stack([u[:, -1], k[:, -1]])
    head = jnp.stack([u[:, 0], k[:, 0]])
    lo = lax.ppermute(last, "space", [(i, i + 1) for i in range(spaces - 1)])
    hi = lax.ppermute(head, "space", [(i + 1, i) for i in range(spaces - 1)])
    cells = pos.reshape(1, -1)
    states, partial = stencil(cells, u, k)
    picked = readings(cells, head, last, lo, hi, partial, params, u.shape[1])
    mine = around_y(picked)
    blocks = mine + [partner(a) for a in mine]

    core = (lax.axis_index("ens") % 2).astype(jnp.int32).reshape(1)
    sums, anomaly = gram(count, core, blocks, noise, values, std, ens_scale)
    lo, sums = lax.optimization_barrier((lo, sums))
    states = add_face(u, k, lo, states, 0)
    sums, states, hi = lax.optimization_barrier((total4(around_z(sums)), states, hi))
    parts = around_x(sums)
    states = add_face(u, k, hi, states, u.shape[1] - 1)
    sums, states = lax.optimization_barrier((total4(parts), states))
    other = partner(sums)
    inv = inverse(sums)
    return update(core, inv, sums, other, anomaly, params), states


def solution(mesh):
    in_specs = (
        P("ens", "space", None, None),
        P("ens", "space", None, None),
        P("space"),
        P("space"),
        P("space"),
        P("space"),
        P("ens", "space"),
        P("ens", "space"),
    )
    out_specs = (P("ens", "space"), P("ens", "space", None, None))
    return jax.shard_map(shards, mesh=mesh, in_specs=in_specs, out_specs=out_specs, check_vma=False)
```
